32 devices in a mesh: lat: 8 (over z, core), lon: 4 (over y, x).
Axes of the slice: x: 2, y: 2, z: 4, core: 2. Of those that a mesh axis runs over, the one named last changes fastest.
Arguments:
- features: bfloat16 [32, 2048, 256], P('lat', 'lon'), may hold values from -6 to 6
- basis: float32 [32, 9, 25], P('lat'), may hold values from -1.2 to 1.2
- span_lo: int32 [32], P('lat'), may hold values from -2 to 0
- span_hi: int32 [32], P('lat'), may hold values from 0 to 2
- weight: bfloat16 [9, 256, 256], replicated, may hold values from -0.125 to 0.125
- cotangent: bfloat16 [32, 2048, 256], P('lat', 'lon'), may hold values from -6 to 6
Outputs:
- mixed: bfloat16 [32, 2048, 256], P('lat', 'lon')
- grad_input: bfloat16 [32, 2048, 256], P('lat', 'lon')
- grad_weight: float32 [9, 256, 256], replicated
The draws below stay inside these ranges and needn't reach their ends.
All inputs are finite; a program needn't handle non-finite values.
Results may differ from the reference program's by a relative error of at most 0.0049.
Values may be sent and summed in bfloat16 or wider, within the bound.
A program may use at most 192 MiB of HBM per device.

```python
import math
import jax
import jax.numpy as jnp

C = 256
K = 9
RAD = 2
TAPS = 25
NLAT = 32
NLON = 2048


def touch_ends(entries, own_key, smallest, top_value):
    longest = entries.shape.index(max(entries.shape))
    spots = []
    for shift in (0, 1):
        where = [jax.random.randint(jax.random.fold_in(own_key, axis), (), 0, length) for axis, length in enumerate(entries.shape)]
        where[longest] = (where[longest] + shift) % entries.shape[longest]
        spots.append(tuple(where))
    return entries.at[spots[0]].set(smallest).at[spots[1]].set(top_value)


def levels(key, extent, shards, smallest, largest):
    level = 1.0
    for dim, parts in shards:
        draws = jax.random.uniform(jax.random.fold_in(jax.random.fold_in(key, 6), dim), (parts,), jnp.float32, smallest / len(shards), largest / len(shards))
        level = level * jnp.repeat(jnp.exp(draws), extent[dim] // parts).reshape((-1,) + (1,) * (len(extent) - 1 - dim))
    return level


def normal_values(key, shape, scale, reach, cuts=(), held_as=jnp.bfloat16):
    values = jax.random.normal(key, shape, jnp.float32) * scale
    if len(cuts) > 0:
        values = levels(key, shape, cuts, -0.22, 0.18) * values
    return jnp.clip(values, min=-reach, max=reach).astype(held_as)


def setup_inputs(seed: int = 0) -> dict:
    key_list = jax.random.split(jax.random.key(seed), 7)
    features = normal_values(key_list[0], (NLAT, NLON, C), 1.0, 6.0, ((0, 8), (1, 4)))
    basis = normal_values(key_list[1], (NLAT, K, TAPS), 0.2, 1.2, ((0, 8),), jnp.float32)
    span_lo = touch_ends(jax.random.randint(key_list[2], (NLAT,), -RAD, 1), jax.random.fold_in(key_list[2], 1), -RAD, 0).astype(jnp.int32)
    span_hi = touch_ends(jax.random.randint(key_list[3], (NLAT,), 0, RAD + 1), jax.random.fold_in(key_list[3], 1), 0, RAD).astype(jnp.int32)
    weight = normal_values(key_list[4], (K, C, C), (K * C) ** -0.5, 0.125)
    cotangent = normal_values(key_list[5], (NLAT, NLON, C), 1.0, 6.0, ((0, 8), (1, 4)))
    return dict(features=features, basis=basis, span_lo=span_lo, span_hi=span_hi, weight=weight, cotangent=cotangent)


def kept_basis(basis, span_lo, span_hi):
    offsets = jnp.arange(TAPS, dtype=jnp.int32) // (2 * RAD + 1) - RAD
    keep = (offsets[None, :] >= span_lo[:, None]) & (offsets[None, :] <= span_hi[:, None])
    return jnp.where(keep[:, None, :], basis, jnp.zeros_like(basis))

def reference(features, basis, span_lo, span_hi, weight, cotangent):
    width = 2 * RAD + 1
    kept = kept_basis(basis, span_lo, span_hi)
    padded = jnp.concatenate([features[:, NLON - RAD:], features, features[:, :RAD]], axis=1)
    padded = jnp.pad(padded, ((RAD, RAD), (0, 0), (0, 0)))
    flat_cot = cotangent.reshape(NLAT * NLON, C)
    mixed = jnp.zeros((NLAT * NLON, C), jnp.float32)
    spread = jnp.zeros((NLAT + 2 * RAD, NLON + 2 * RAD, C), jnp.float32)
    grads = []
    for kernel in range(K):
        total = jnp.zeros((NLAT, NLON, C), jnp.float32)
        for tap_index in range(TAPS):
            row_shift = tap_index // width - RAD
            col_shift = tap_index % width - RAD
            window = padded[RAD + row_shift:RAD + row_shift + NLAT, RAD + col_shift:RAD + col_shift + NLON]
            total = total + kept[:, kernel, tap_index][:, None, None] * window.astype(jnp.float32)
        plane = total.astype(jnp.bfloat16).reshape(NLAT * NLON, C)
        mixed = mixed + jnp.dot(plane, weight[kernel], preferred_element_type=jnp.float32)
        grads.append(jnp.dot(plane.T, flat_cot, preferred_element_type=jnp.float32))
        grad_plane = jnp.dot(flat_cot, weight[kernel].T, preferred_element_type=jnp.float32)
        grad_plane = grad_plane.astype(jnp.bfloat16).reshape(NLAT, NLON, C).astype(jnp.float32)
        for tap_index in range(TAPS):
            row_shift = tap_index // width - RAD
            col_shift = tap_index % width - RAD
            spread = spread.at[RAD + row_shift:RAD + row_shift + NLAT, RAD + col_shift:RAD + col_shift + NLON].add(kept[:, kernel, tap_index][:, None, None] * grad_plane)
    middle = spread[RAD:RAD + NLAT]
    grad_input = middle[:, RAD:RAD + NLON]
    grad_input = grad_input.at[:, NLON - RAD:].add(middle[:, :RAD])
    grad_input = grad_input.at[:, :RAD].add(middle[:, NLON + RAD:])
    scale = 1.0 / math.sqrt(NLAT * NLON)
    grad_weight = jnp.stack(grads) * scale
    return (mixed.astype(jnp.bfloat16).reshape(NLAT, NLON, C), grad_input.astype(jnp.bfloat16), grad_weight)
```

```python
import functools
import math

import jax
import jax.numpy as jnp
from jax import lax
from jax.experimental import pallas as pl
from jax.experimental.pallas import tpu as pltpu
from jax.sharding import PartitionSpec as P

K = 9
RAD = 2
WIDTH = 2 * RAD + 1
TAPS = WIDTH * WIDTH
J = 32
EDGE = 8
WIN = J + 2 * EDGE


def passed(block, axis, step, periodic):
    count = lax.axis_size(axis)
    route = [(i, (i + step) % count) for i in range(count) if periodic or 0 <= i + step < count]
    return lax.ppermute(block, axis, route)


def extended(block):
    lon_count = block.shape[1]
    low = passed(block[:, lon_count - EDGE :], "lon", 1, True)
    high = passed(block[:, :EDGE], "lon", -1, True)
    block = jnp.concatenate([low, block, high], axis=1)
    above = passed(block[block.shape[0] - RAD :], "lat", 1, False)
    below = passed(block[:RAD], "lat", -1, False)
    return jnp.concatenate([above, block, below], axis=0)


def kept_basis(basis, span_lo, span_hi):
    offsets = jnp.arange(TAPS, dtype=jnp.int32) // WIDTH - RAD
    keep = (offsets[None, :] >= span_lo[:, None]) & (offsets[None, :] <= span_hi[:, None])
    return jnp.where(keep[:, None, :], basis, jnp.zeros_like(basis))


def banded(coef):
    rows = coef.shape[0]
    lane = jnp.arange(WIDTH * WIN)
    spread = jnp.repeat(coef.astype(jnp.bfloat16), WIN, axis=2)
    where_col = lane[None, :] % WIN - jnp.arange(J)[:, None] - (EDGE - RAD)
    out = jnp.zeros((rows, K, J, WIDTH * WIN), jnp.bfloat16)
    for e in range(WIDTH):
        out = jnp.where((where_col == e)[None, None], spread[:, :, None, :, e], out)
    return out.reshape(rows, K * J, WIDTH * WIN)


def kernel(scale, tile, f_ref, c_ref, cot_ref, fa_ref, ca_ref, w_ref, wt_ref, mixed_ref, gi_ref, gw_ref, y_ref, z_ref, acc_ref):
    rows, lon_count, channels = cot_ref.shape
    tiles = lon_count // tile
    acc_ref[...] = jnp.zeros_like(acc_ref)

    def stencil(x_ref, a_ref, out_ref, i, start):
        a = a_ref[i]
        for b in range(tile // J):
            first = pl.multiple_of(start + b * J, J)
            x = x_ref[pl.ds(i, WIDTH), pl.ds(first, WIN), :].reshape(WIDTH * WIN, channels)
            y = jnp.dot(a, x, preferred_element_type=jnp.float32).astype(jnp.bfloat16)
            for k in range(K):
                out_ref[b * J : (b + 1) * J, k * channels : (k + 1) * channels] = y[k * J : (k + 1) * J]

    def step(s, carry):
        i = s // tiles
        start = pl.multiple_of((s % tiles) * tile, tile)
        here = pl.ds(start, tile)
        stencil(f_ref, fa_ref, y_ref, i, start)
        stencil(c_ref, ca_ref, z_ref, i, start)
        mixed_ref[i, here, :] = jnp.dot(
            y_ref[...], w_ref[...], preferred_element_type=jnp.float32
        ).astype(jnp.bfloat16)
        acc_ref[...] += jnp.dot(cot_ref[i, here, :].T, y_ref[...], preferred_element_type=jnp.float32)
        gi_ref[i, here, :] = jnp.dot(
            z_ref[...], wt_ref[...], preferred_element_type=jnp.float32
        ).astype(jnp.bfloat16)
        return carry

    lax.fori_loop(0, rows * tiles, step, 0)
    for k in range(K):
        gw_ref[k] = acc_ref[:, k * channels : (k + 1) * channels].T * scale


def per_device(features, basis, span_lo, span_hi, weight, cotangent):
    rows, lon_count, channels = features.shape
    kept = kept_basis(basis, span_lo, span_hi)
    above = passed(kept[rows - RAD :], "lat", 1, False)
    below = passed(kept[:RAD], "lat", -1, False)
    kept_ext = jnp.concatenate([above, kept, below], axis=0).reshape(rows + 2 * RAD, K, WIDTH, WIDTH)
    forward = banded(kept_ext[RAD : RAD + rows])
    flipped = kept_ext[:, :, ::-1, ::-1]
    adjoint = banded(jnp.stack([flipped[r : r + rows, :, r] for r in range(WIDTH)], axis=2))
    f_ext = extended(features)
    c_ext = extended(cotangent)
    w = weight.reshape(K * channels, channels)
    wt = jnp.swapaxes(weight, 1, 2).reshape(K * channels, channels)
    scale = 1.0 / math.sqrt(rows * lax.axis_size("lat") * lon_count * lax.axis_size("lon"))
    tile = 512
    mixed, grad_input, local = pl.pallas_call(
        functools.partial(kernel, scale, tile),
        out_shape=(
            jax.ShapeDtypeStruct(features.shape, jnp.bfloat16),
            jax.ShapeDtypeStruct(features.shape, jnp.bfloat16),
            jax.ShapeDtypeStruct(weight.shape, jnp.float32),
        ),
        in_specs=[pl.BlockSpec(memory_space=pltpu.VMEM)] * 7,
        out_specs=[pl.BlockSpec(memory_space=pltpu.VMEM)] * 3,
        scratch_shapes=[
            pltpu.VMEM((tile, K * channels), jnp.bfloat16),
            pltpu.VMEM((tile, K * channels), jnp.bfloat16),
            pltpu.VMEM((channels, K * channels), jnp.float32),
        ],
        compiler_params=pltpu.CompilerParams(vmem_limit_bytes=50 * 2**20),
    )(f_ext, c_ext, cotangent, forward, adjoint, w, wt)
    return (mixed, grad_input, lax.psum(local, ("lat", "lon")))


def solution(mesh):
    return jax.shard_map(
        per_device,
        mesh=mesh,
        in_specs=(
            P("lat", "lon", None),
            P("lat", None, None),
            P("lat"),
            P("lat"),
            P(),
            P("lat", "lon", None),
        ),
        out_specs=(P("lat", "lon", None), P("lat", "lon", None), P()),
        check_vma=False,
    )
```

```python
import functools
import math

import jax
import jax.numpy as jnp
from jax import lax
from jax.experimental import pallas as pl
from jax.experimental.pallas import tpu as pltpu
from jax.sharding import PartitionSpec as P

K = 9
RAD = 2
WIDTH = 2 * RAD + 1
TAPS = WIDTH * WIDTH
J = 32
EDGE = 8
WIN = J + 2 * EDGE
SUB, LANES = 16, 128
MESH = pl.DeviceIdType.MESH


def passed(block, axis, step, periodic):
    count = lax.axis_size(axis)
    route = [(i, (i + step) % count) for i in range(count) if periodic or 0 <= i + step < count]
    return lax.ppermute(block, axis, route)


def extended(block):
    lon_count = block.shape[1]
    low = passed(block[:, lon_count - EDGE :], "lon", 1, True)
    high = passed(block[:, :EDGE], "lon", -1, True)
    block = jnp.concatenate([low, block, high], axis=1)
    above = passed(block[block.shape[0] - RAD :], "lat", 1, False)
    below = passed(block[:RAD], "lat", -1, False)
    return jnp.concatenate([above, block, below], axis=0)


def kept_basis(basis, span_lo, span_hi):
    offsets = jnp.arange(TAPS, dtype=jnp.int32) // WIDTH - RAD
    keep = (offsets[None, :] >= span_lo[:, None]) & (offsets[None, :] <= span_hi[:, None])
    return jnp.where(keep[:, None, :], basis, jnp.zeros_like(basis))


def banded(coef):
    rows = coef.shape[0]
    lane = jnp.arange(WIDTH * WIN)
    spread = jnp.repeat(coef.astype(jnp.bfloat16), WIN, axis=2)
    where_col = lane[None, :] % WIN - jnp.arange(J)[:, None] - (EDGE - RAD)
    out = jnp.zeros((rows, K, J, WIDTH * WIN), jnp.bfloat16)
    for e in range(WIDTH):
        out = jnp.where((where_col == e)[None, None], spread[:, :, None, :, e], out)
    return out.reshape(rows, K * J, WIDTH * WIN)


def kernel(scale, tile, f_ref, c_ref, cot_ref, fa_ref, ca_ref, w_ref, wt_ref, mixed_ref, gi_ref, gw_ref, y_ref, z_ref, acc_ref):
    rows, lon_count, channels = cot_ref.shape
    tiles = lon_count // tile
    acc_ref[...] = jnp.zeros_like(acc_ref)

    def stencil(x_ref, a_ref, out_ref, i, start):
        a = a_ref[i]
        for b in range(tile // J):
            first = pl.multiple_of(start + b * J, J)
            x = x_ref[pl.ds(i, WIDTH), pl.ds(first, WIN), :].reshape(WIDTH * WIN, channels)
            y = jnp.dot(a, x, preferred_element_type=jnp.float32).astype(jnp.bfloat16)
            for k in range(K):
                out_ref[b * J : (b + 1) * J, k * channels : (k + 1) * channels] = y[k * J : (k + 1) * J]

    def step(s, carry):
        i = s // tiles
        start = pl.multiple_of((s % tiles) * tile, tile)
        here = pl.ds(start, tile)
        stencil(f_ref, fa_ref, y_ref, i, start)
        stencil(c_ref, ca_ref, z_ref, i, start)
        mixed_ref[i, here, :] = jnp.dot(
            y_ref[...], w_ref[...], preferred_element_type=jnp.float32
        ).astype(jnp.bfloat16)
        acc_ref[...] += jnp.dot(cot_ref[i, here, :].T, y_ref[...], preferred_element_type=jnp.float32)
        gi_ref[i, here, :] = jnp.dot(
            z_ref[...], wt_ref[...], preferred_element_type=jnp.float32
        ).astype(jnp.bfloat16)
        return carry

    lax.fori_loop(0, rows * tiles, step, 0)
    per = channels // SUB
    for k in range(K):
        turned = acc_ref[:, k * channels : (k + 1) * channels].T * scale
        for h in range(channels // LANES):
            first = (k * (channels // LANES) + h) * per
            block = turned[:, h * LANES : (h + 1) * LANES]
            gw_ref[first : first + per] = block.reshape(per, SUB, LANES)
    used = K * per * (channels // LANES)
    if gw_ref.shape[0] > used:
        gw_ref[used:] = jnp.zeros((gw_ref.shape[0] - used, SUB, LANES), jnp.float32)


def reduce_kernel(
    lon, pairs, q, in_ref, out_ref, got_a, send_b, got_b, part, send_c, got_c,
    a_send, a_recv, b_send, b_recv, c_send, c_recv, d_send, d_recv, e_send, e_recv, f_send, f_recv,
):
    lat = lax.axis_index("lat")
    n = lax.axis_index("lon")
    core, z = lax.rem(lat, 2), lat // 2
    partner = (lat + 1 - 2 * core, n)
    piece = pairs * q
    half = lon * piece

    def lon_peer(s):
        return lax.rem(n + s, lon)

    def pair_peer(s):
        return lax.rem(z + s, pairs)

    barrier = pltpu.get_barrier_semaphore()
    pl.semaphore_signal(barrier, inc=1, device_id=partner, device_id_type=MESH)
    for s in range(1, lon):
        pl.semaphore_signal(barrier, inc=1, device_id=(lat, lon_peer(s)), device_id_type=MESH)
    for s in range(1, pairs):
        pl.semaphore_signal(
            barrier, inc=1, device_id=(pair_peer(s) * 2 + core, n), device_id_type=MESH
        )
    pl.semaphore_wait(barrier, 1 + lon - 1 + pairs - 1)

    def remote(src, dst, send, recv, device):
        copy = pltpu.make_async_remote_copy(
            src_ref=src, dst_ref=dst, send_sem=send, recv_sem=recv,
            device_id=device, device_id_type=MESH,
        )
        copy.start()
        return copy

    theirs, mine = (1 - core) * half, core * half
    a_copies = []
    for s in range(lon):
        p = lon_peer(s + 1)
        a_copies.append(
            remote(
                in_ref.at[pl.ds(theirs + p * piece, piece)],
                got_a.at[pl.ds(p * piece, piece)],
                a_send.at[s], a_recv.at[s], partner,
            )
        )
    b_copies = []
    for s in range(lon):
        p = lon_peer(s + 1)
        a_copies[s].wait_recv()
        total = in_ref[pl.ds(mine + p * piece, piece)] + got_a[pl.ds(p * piece, piece)]
        if s < lon - 1:
            send_b[s] = total.astype(jnp.bfloat16)
            b_copies.append(remote(send_b.at[s], got_b.at[s], b_send.at[s], b_recv.at[s], (lat, p)))
        else:
            part[...] = total
    for s in range(lon - 1):
        b_copies[s].wait_recv()
        part[...] += got_b[s].astype(jnp.float32)
    c_copies = []
    for s in range(pairs - 1):
        p = pair_peer(s + 1)
        send_c[s] = part[pl.ds(p * q, q)].astype(jnp.bfloat16)
        c_copies.append(
            remote(send_c.at[s], got_c.at[s], c_send.at[s], c_recv.at[s], (p * 2 + core, n))
        )
    total = part[pl.ds(z * q, q)]
    for s in range(pairs - 1):
        c_copies[s].wait_recv()
        total = total + got_c[s].astype(jnp.float32)
    own = mine + n * piece
    out_ref[pl.ds(own + z * q, q)] = total.astype(jnp.bfloat16)

    d_copies, e_copies, f_copies = [], [], []

    def to_lon(t):
        src = out_ref.at[pl.ds(own + lax.rem(z + pairs - t, pairs) * q, q)]
        for s in range(lon - 1):
            e_copies.append(
                remote(src, src, e_send.at[t, s], e_recv.at[t, s], (lat, lon_peer(s + 1)))
            )

    def to_partner(s, p):
        src = out_ref.at[pl.ds(mine + p * piece, piece)]
        f_copies.append(remote(src, src, f_send.at[s], f_recv.at[s], partner))

    src = out_ref.at[pl.ds(own + z * q, q)]
    for s in range(pairs - 1):
        d_copies.append(
            remote(src, src, d_send.at[s], d_recv.at[s], (pair_peer(s + 1) * 2 + core, n))
        )
    to_lon(0)
    for t in range(1, pairs):
        d_copies[t - 1].wait_recv()
        to_lon(t)
    to_partner(0, n)
    for s in range(lon - 1):
        for t in range(pairs):
            e_copies[t * (lon - 1) + s].wait_recv()
        to_partner(s + 1, lax.rem(n + lon - s - 1, lon))
    for copy in f_copies:
        copy.wait_recv()
    for copy in a_copies + b_copies + c_copies + d_copies + e_copies + f_copies:
        copy.wait_send()


def summed(local, lon, pairs, q):
    groups = local.shape[0]
    piece = pairs * q
    dma = pltpu.SemaphoreType.DMA
    bf16, f32 = jnp.bfloat16, jnp.float32
    return pl.pallas_call(
        functools.partial(reduce_kernel, lon, pairs, q),
        out_shape=jax.ShapeDtypeStruct((groups, SUB, LANES), bf16),
        in_specs=[pl.BlockSpec(memory_space=pltpu.VMEM)],
        out_specs=pl.BlockSpec(memory_space=pltpu.VMEM),
        scratch_shapes=[
            pltpu.VMEM((lon * piece, SUB, LANES), f32),
            pltpu.VMEM((lon - 1, piece, SUB, LANES), bf16),
            pltpu.VMEM((lon - 1, piece, SUB, LANES), bf16),
            pltpu.VMEM((piece, SUB, LANES), f32),
            pltpu.VMEM((pairs - 1, q, SUB, LANES), bf16),
            pltpu.VMEM((pairs - 1, q, SUB, LANES), bf16),
            dma((lon,)), dma((lon,)),
            dma((lon - 1,)), dma((lon - 1,)),
            dma((pairs - 1,)), dma((pairs - 1,)),
            dma((pairs - 1,)), dma((pairs - 1,)),
            dma((pairs, lon - 1)), dma((pairs, lon - 1)),
            dma((lon,)), dma((lon,)),
        ],
        compiler_params=pltpu.CompilerParams(
            collective_id=1, has_side_effects=True, vmem_limit_bytes=40 * 2**20
        ),
    )(local)


def per_device(features, basis, span_lo, span_hi, weight, cotangent):
    rows, lon_count, channels = features.shape
    kept = kept_basis(basis, span_lo, span_hi)
    above = passed(kept[rows - RAD :], "lat", 1, False)
    below = passed(kept[:RAD], "lat", -1, False)
    kept_ext = jnp.concatenate([above, kept, below], axis=0).reshape(rows + 2 * RAD, K, WIDTH, WIDTH)
    forward = banded(kept_ext[RAD : RAD + rows])
    flipped = kept_ext[:, :, ::-1, ::-1]
    adjoint = banded(jnp.stack([flipped[r : r + rows, :, r] for r in range(WIDTH)], axis=2))
    f_ext = extended(features)
    c_ext = extended(cotangent)
    w = weight.reshape(K * channels, channels)
    wt = jnp.swapaxes(weight, 1, 2).reshape(K * channels, channels)
    scale = 1.0 / math.sqrt(rows * lax.axis_size("lat") * lon_count * lax.axis_size("lon"))
    tile = 512
    lon, pairs = lax.axis_size("lon"), lax.axis_size("lat") // 2
    used = weight.size // (SUB * LANES)
    q = -(-used // (2 * lon * pairs))
    mixed, grad_input, local = pl.pallas_call(
        functools.partial(kernel, scale, tile),
        out_shape=(
            jax.ShapeDtypeStruct(features.shape, jnp.bfloat16),
            jax.ShapeDtypeStruct(features.shape, jnp.bfloat16),
            jax.ShapeDtypeStruct((2 * lon * pairs * q, SUB, LANES), jnp.float32),
        ),
        in_specs=[pl.BlockSpec(memory_space=pltpu.VMEM)] * 7,
        out_specs=[pl.BlockSpec(memory_space=pltpu.VMEM)] * 3,
        scratch_shapes=[
            pltpu.VMEM((tile, K * channels), jnp.bfloat16),
            pltpu.VMEM((tile, K * channels), jnp.bfloat16),
            pltpu.VMEM((channels, K * channels), jnp.float32),
        ],
        compiler_params=pltpu.CompilerParams(vmem_limit_bytes=50 * 2**20),
    )(f_ext, c_ext, cotangent, forward, adjoint, w, wt)
    total = summed(local, lon, pairs, q)[:used].astype(jnp.float32)
    total = total.reshape(K, channels // LANES, channels, LANES)
    grad_weight = jnp.swapaxes(total, 1, 2).reshape(weight.shape)
    return (mixed, grad_input, grad_weight)


def solution(mesh):
    return jax.shard_map(
        per_device,
        mesh=mesh,
        in_specs=(
            P("lat", "lon", None),
            P("lat", None, None),
            P("lat"),
            P("lat"),
            P(),
            P("lat", "lon", None),
        ),
        out_specs=(P("lat", "lon", None), P("lat", "lon", None), P()),
        check_vma=False,
    )
```

```python
import functools
import math

import jax
import jax.numpy as jnp
from jax import lax
from jax.experimental import pallas as pl
from jax.experimental.pallas import tpu as pltpu
from jax.sharding import PartitionSpec as P

K = 9
RAD = 2
WIDTH = 2 * RAD + 1
TAPS = WIDTH * WIDTH
J = 32
EDGE = 8
PAD = 16
WIN = J + 2 * EDGE
SUB, LANES = 16, 128
MESH = pl.DeviceIdType.MESH


def kept_basis(basis, span_lo, span_hi):
    offsets = jnp.arange(TAPS, dtype=jnp.int32) // WIDTH - RAD
    keep = (offsets[None, :] >= span_lo[:, None]) & (offsets[None, :] <= span_hi[:, None])
    return jnp.where(keep[:, None, :], basis, jnp.zeros_like(basis))


def remote(src, dst, send, recv, device):
    copy = pltpu.make_async_remote_copy(
        src_ref=src, dst_ref=dst, send_sem=send, recv_sem=recv,
        device_id=device, device_id_type=MESH,
    )
    copy.start()
    return copy


def reduce_steps(
    lon, pairs, q, in_ref, out_ref, got_a, send_b, got_b, part, send_c, got_c,
    a_send, a_recv, b_send, b_recv, c_send, c_recv, d_send, d_recv, e_send, e_recv, f_send, f_recv,
):
    lat = lax.axis_index("lat")
    n = lax.axis_index("lon")
    core, z = lax.rem(lat, 2), lat // 2
    partner = (lat + 1 - 2 * core, n)
    piece = pairs * q
    half = lon * piece

    def lon_peer(s):
        return lax.rem(n + s, lon)

    def pair_peer(s):
        return lax.rem(z + s, pairs)

    theirs, mine = (1 - core) * half, core * half
    a_copies = []
    for s in range(lon):
        p = lon_peer(s + 1)
        a_copies.append(
            remote(
                in_ref.at[pl.ds(theirs + p * piece, piece)],
                got_a.at[pl.ds(p * piece, piece)],
                a_send.at[s], a_recv.at[s], partner,
            )
        )
    yield
    b_copies = []
    for s in range(lon):
        p = lon_peer(s + 1)
        a_copies[s].wait_recv()
        total = in_ref[pl.ds(mine + p * piece, piece)] + got_a[pl.ds(p * piece, piece)]
        if s < lon - 1:
            send_b[s] = total.astype(jnp.bfloat16)
            b_copies.append(remote(send_b.at[s], got_b.at[s], b_send.at[s], b_recv.at[s], (lat, p)))
        else:
            part[...] = total
    yield
    for s in range(lon - 1):
        b_copies[s].wait_recv()
        part[...] += got_b[s].astype(jnp.float32)
    c_copies = []
    for s in range(pairs - 1):
        p = pair_peer(s + 1)
        send_c[s] = part[pl.ds(p * q, q)].astype(jnp.bfloat16)
        c_copies.append(
            remote(send_c.at[s], got_c.at[s], c_send.at[s], c_recv.at[s], (p * 2 + core, n))
        )
    yield
    total = part[pl.ds(z * q, q)]
    for s in range(pairs - 1):
        c_copies[s].wait_recv()
        total = total + got_c[s].astype(jnp.float32)
    own = mine + n * piece
    out_ref[pl.ds(own + z * q, q)] = total.astype(jnp.bfloat16)

    d_copies, e_copies, f_copies = [], [], []

    def to_lon(t):
        src = out_ref.at[pl.ds(own + lax.rem(z + pairs - t, pairs) * q, q)]
        for s in range(lon - 1):
            e_copies.append(
                remote(src, src, e_send.at[t, s], e_recv.at[t, s], (lat, lon_peer(s + 1)))
            )

    def to_partner(s, p):
        src = out_ref.at[pl.ds(mine + p * piece, piece)]
        f_copies.append(remote(src, src, f_send.at[s], f_recv.at[s], partner))

    src = out_ref.at[pl.ds(own + z * q, q)]
    for s in range(pairs - 1):
        d_copies.append(
            remote(src, src, d_send.at[s], d_recv.at[s], (pair_peer(s + 1) * 2 + core, n))
        )
    to_lon(0)
    yield
    for t in range(1, pairs):
        d_copies[t - 1].wait_recv()
        to_lon(t)
    to_partner(0, n)
    yield
    for s in range(lon - 1):
        for t in range(pairs):
            e_copies[t * (lon - 1) + s].wait_recv()
        to_partner(s + 1, lax.rem(n + lon - s - 1, lon))
    for copy in f_copies:
        copy.wait_recv()
    for copy in a_copies + b_copies + c_copies + d_copies + e_copies + f_copies:
        copy.wait_send()


def halo_starts(src_ref, dst_ref, send, recv):
    rows, cols = src_ref.shape[0], src_ref.shape[1]
    lat, n = lax.axis_index("lat"), lax.axis_index("lon")
    lats, lons = lax.axis_size("lat"), lax.axis_size("lon")
    sides = {
        1: (pl.ds(rows - RAD, RAD), pl.ds(0, RAD)),
        0: (pl.ds(0, rows), pl.ds(RAD, rows)),
        -1: (pl.ds(0, RAD), pl.ds(RAD + rows, RAD)),
    }
    spans = {
        1: (pl.ds(cols - PAD, PAD), pl.ds(0, PAD)),
        0: (pl.ds(0, cols), pl.ds(PAD, cols)),
        -1: (pl.ds(0, PAD), pl.ds(PAD + cols, PAD)),
    }
    present = {1: lat < lats - 1, -1: lat > 0}
    copies = {1: [], 0: [], -1: []}
    for dy in (1, -1, 0):
        for dx in (0, 1, -1):
            if dy == 0 and dx == 0:
                continue
            slot = (dy + 1) * 3 + dx + 1
            copies[dy].append(
                pltpu.make_async_remote_copy(
                    src_ref=src_ref.at[sides[dy][0], spans[dx][0]],
                    dst_ref=dst_ref.at[sides[dy][1], spans[dx][1]],
                    send_sem=send.at[slot], recv_sem=recv.at[slot],
                    device_id=(lat + dy, lax.rem(n + dx + lons, lons)), device_id_type=MESH,
                )
            )
    for dy in (1, -1):
        @pl.when(present[dy])
        def _():
            for copy in copies[dy]:
                copy.start()
    for copy in copies[0]:
        copy.start()

    def received():
        for copy in copies[0]:
            copy.wait_recv()
        for dy in (1, -1):
            @pl.when(present[-dy])
            def _():
                for copy in copies[dy]:
                    copy.wait_recv()

    def sent():
        for copy in copies[0]:
            copy.wait_send()
        for dy in (1, -1):
            @pl.when(present[dy])
            def _():
                for copy in copies[dy]:
                    copy.wait_send()

    return received, sent


def kernel(
    scale, tile, lon, pairs, q, f_ref, c_ref, b_ref, w_hbm, mixed_ref, gi_ref, gw_ref,
    fx, cx, bx, w_ref, wt_ref, v_ref, u_ref, fa_ref, ca_ref, y_ref, acc_ref, groups_ref,
    local_sem, f_send, f_recv, c_send, c_recv, b_send, b_recv, *reduce_scratch,
):
    rows, lon_count, channels = f_ref.shape
    tiles = lon_count // tile
    lat, n = lax.axis_index("lat"), lax.axis_index("lon")
    lats = lax.axis_size("lat")
    core, z = lax.rem(lat, 2), lat // 2
    has = {1: lat < lats - 1, -1: lat > 0}

    barrier = pltpu.get_barrier_semaphore()
    for dy in (1, -1):
        @pl.when(has[dy])
        def _():
            for dx in (-1, 0, 1):
                there = (lat + dy, lax.rem(n + dx + lon, lon))
                pl.semaphore_signal(barrier, inc=1, device_id=there, device_id_type=MESH)
    for s in range(1, lon):
        there = (lat, lax.rem(n + s, lon))
        pl.semaphore_signal(barrier, inc=1, device_id=there, device_id_type=MESH)
    for s in range(1, pairs):
        there = (lax.rem(z + s, pairs) * 2 + core, n)
        pl.semaphore_signal(barrier, inc=1, device_id=there, device_id_type=MESH)
    here = pl.ds(RAD, rows)
    middle = pl.ds(PAD, lon_count)
    locals_ = [
        pltpu.make_async_copy(f_ref, fx.at[here, middle], local_sem.at[0]),
        pltpu.make_async_copy(c_ref, cx.at[here, middle], local_sem.at[1]),
        pltpu.make_async_copy(w_hbm, w_ref, local_sem.at[2]),
    ]
    for copy in locals_:
        copy.start()
    bx[here] = b_ref[...]
    for dy, edge in ((1, 0), (-1, RAD + rows)):
        @pl.when(jnp.logical_not(has[-dy]))
        def _():
            fx[edge : edge + RAD] = jnp.zeros((RAD,) + fx.shape[1:], jnp.bfloat16)
            cx[edge : edge + RAD] = jnp.zeros((RAD,) + cx.shape[1:], jnp.bfloat16)
            bx[edge : edge + RAD] = jnp.zeros((RAD,) + bx.shape[1:], jnp.float32)
    pl.semaphore_wait(
        barrier,
        3 * has[1].astype(jnp.int32) + 3 * has[-1].astype(jnp.int32) + lon - 1 + pairs - 1,
    )

    b_copies = {}
    for slot, dy, src, dst in ((0, 1, rows - RAD, 0), (1, -1, 0, RAD + rows)):
        b_copies[dy] = pltpu.make_async_remote_copy(
            src_ref=b_ref.at[pl.ds(src, RAD)], dst_ref=bx.at[pl.ds(dst, RAD)],
            send_sem=b_send.at[slot], recv_sem=b_recv.at[slot],
            device_id=(lat + dy, n), device_id_type=MESH,
        )

        @pl.when(has[dy])
        def _():
            b_copies[dy].start()
    f_received, f_sent = halo_starts(f_ref, fx, f_send, f_recv)
    c_received, c_sent = halo_starts(c_ref, cx, c_send, c_recv)

    locals_[2].wait()
    for k in range(K):
        block = slice(k * channels, (k + 1) * channels)
        wt_ref[block] = w_ref[block].T

    for dy in (1, -1):
        @pl.when(has[-dy])
        def _():
            b_copies[dy].wait_recv()
    taps = lax.broadcasted_iota(jnp.int32, (LANES, 256), 0)
    lane = lax.broadcasted_iota(jnp.int32, (LANES, 256), 1)

    def segment(lanes):
        return sum((lanes >= m * WIN).astype(jnp.int32) for m in range(1, WIDTH))

    seg = segment(lane)
    coef = bx[...].astype(jnp.bfloat16).reshape((rows + 2 * RAD) * SUB, LANES)

    def pick(want):
        chosen = jnp.where(taps == want, 1.0, 0.0).astype(jnp.bfloat16)
        out = jnp.dot(coef, chosen, preferred_element_type=jnp.float32)
        return out.reshape(rows + 2 * RAD, SUB, 256)

    for e in range(WIDTH):
        v_ref[e] = pick(seg * WIDTH + e)
        u_ref[e] = pick((WIDTH - 1 - seg) * WIDTH + WIDTH - 1 - e)
    lane = lax.broadcasted_iota(jnp.int32, (J, 256), 1)
    seg_j = segment(lane)
    col = lane - seg_j * WIN - lax.broadcasted_iota(jnp.int32, (J, 256), 0) - (EDGE - RAD)
    seg_k = segment(lax.broadcasted_iota(jnp.int32, (SUB, 256), 1))

    def build(i, carry):
        adjoint = []
        for e in range(WIDTH):
            line = u_ref[e, i]
            for r in range(1, WIDTH):
                line = jnp.where(seg_k == r, u_ref[e, i + r], line)
            adjoint.append(line)
        forward = [v_ref[e, i + RAD] for e in range(WIDTH)]
        for lines, a_ref in ((forward, fa_ref), (adjoint, ca_ref)):
            for k in range(K):
                a = jnp.zeros((J, 256), jnp.float32)
                for e in range(WIDTH):
                    a = jnp.where(col == e, jnp.broadcast_to(lines[e][k : k + 1], (J, 256)), a)
                a_ref[i, k * J : (k + 1) * J] = a.astype(jnp.bfloat16)
        return carry

    lax.fori_loop(0, rows, build, 0)
    acc_ref[...] = jnp.zeros_like(acc_ref)

    def stencil(x_ref, a_ref, i, start):
        a = a_ref[i][:, : WIDTH * WIN]
        for b in range(tile // J):
            first = pl.multiple_of(start + b * J, PAD)
            x = x_ref[pl.ds(i, WIDTH), pl.ds(first, J + 2 * PAD), :]
            x = x[:, PAD - EDGE : PAD - EDGE + WIN].reshape(WIDTH * WIN, channels)
            y = jnp.dot(a, x, preferred_element_type=jnp.float32).astype(jnp.bfloat16)
            for k in range(K):
                y_ref[b * J : (b + 1) * J, k * channels : (k + 1) * channels] = y[k * J : (k + 1) * J]

    def forward_step(s, carry):
        i = s // tiles
        start = pl.multiple_of((s % tiles) * tile, tile)
        stencil(fx, fa_ref, i, start)
        mixed_ref[i, pl.ds(start, tile), :] = jnp.dot(
            y_ref[...], w_ref[...], preferred_element_type=jnp.float32
        ).astype(jnp.bfloat16)
        cot = cx[i + RAD, pl.ds(pl.multiple_of(start + PAD, PAD), tile), :]
        acc_ref[...] += jnp.dot(cot.T, y_ref[...], preferred_element_type=jnp.float32)
        return carry

    def adjoint_step(s, carry):
        i = s // tiles
        start = pl.multiple_of((s % tiles) * tile, tile)
        stencil(cx, ca_ref, i, start)
        gi_ref[i, pl.ds(start, tile), :] = jnp.dot(
            y_ref[...], wt_ref[...], preferred_element_type=jnp.float32
        ).astype(jnp.bfloat16)
        return carry

    locals_[0].wait()
    locals_[1].wait()
    f_received()
    lax.fori_loop(0, rows * tiles, forward_step, 0)
    per = channels // SUB
    for k in range(K):
        turned = acc_ref[:, k * channels : (k + 1) * channels].T * scale
        for h in range(channels // LANES):
            first = (k * (channels // LANES) + h) * per
            block = turned[:, h * LANES : (h + 1) * LANES]
            groups_ref[first : first + per] = block.reshape(per, SUB, LANES)
    used = K * per * (channels // LANES)
    if groups_ref.shape[0] > used:
        groups_ref[used:] = jnp.zeros((groups_ref.shape[0] - used, SUB, LANES), jnp.float32)

    reduction = reduce_steps(lon, pairs, q, groups_ref, gw_ref, *reduce_scratch)
    next(reduction)
    c_received()
    steps = rows * tiles
    cuts = [0, max(1, steps // 4), max(1, steps * 3 // 4), steps]
    for lo, hi in zip(cuts[:-1], cuts[1:]):
        lax.fori_loop(lo, hi, adjoint_step, 0)
        next(reduction)
    for _ in reduction:
        pass
    f_sent()
    c_sent()
    for dy in (1, -1):
        @pl.when(has[dy])
        def _():
            b_copies[dy].wait_send()


def per_device(features, basis, span_lo, span_hi, weight, cotangent):
    rows, lon_count, channels = features.shape
    kept = kept_basis(basis, span_lo, span_hi)
    coef = jnp.pad(kept, ((0, 0), (0, SUB - K), (0, LANES - TAPS)))
    scale = 1.0 / math.sqrt(rows * lax.axis_size("lat") * lon_count * lax.axis_size("lon"))
    tile = 512
    lon, pairs = lax.axis_size("lon"), lax.axis_size("lat") // 2
    used = weight.size // (SUB * LANES)
    q = -(-used // (2 * lon * pairs))
    piece = pairs * q
    groups = 2 * lon * piece
    dma = pltpu.SemaphoreType.DMA
    bf16, f32 = jnp.bfloat16, jnp.float32
    vmem = pl.BlockSpec(memory_space=pltpu.VMEM)
    anywhere = pl.BlockSpec(memory_space=pl.ANY)
    wide = (rows + 2 * RAD, lon_count + 2 * PAD, channels)
    mixed, grad_input, total = pl.pallas_call(
        functools.partial(kernel, scale, tile, lon, pairs, q),
        out_shape=(
            jax.ShapeDtypeStruct(features.shape, bf16),
            jax.ShapeDtypeStruct(features.shape, bf16),
            jax.ShapeDtypeStruct((groups, SUB, LANES), bf16),
        ),
        in_specs=[anywhere, anywhere, vmem, anywhere],
        out_specs=[vmem] * 3,
        scratch_shapes=[
            pltpu.VMEM(wide, bf16),
            pltpu.VMEM(wide, bf16),
            pltpu.VMEM((rows + 2 * RAD, SUB, LANES), f32),
            pltpu.VMEM((K * channels, channels), bf16),
            pltpu.VMEM((K * channels, channels), bf16),
            pltpu.VMEM((WIDTH, rows + 2 * RAD, SUB, 256), f32),
            pltpu.VMEM((WIDTH, rows + 2 * RAD, SUB, 256), f32),
            pltpu.VMEM((rows, K * J, 256), bf16),
            pltpu.VMEM((rows, K * J, 256), bf16),
            pltpu.VMEM((tile, K * channels), bf16),
            pltpu.VMEM((channels, K * channels), f32),
            pltpu.VMEM((groups, SUB, LANES), f32),
            dma((3,)), dma((9,)), dma((9,)), dma((9,)), dma((9,)), dma((2,)), dma((2,)),
            pltpu.VMEM((lon * piece, SUB, LANES), f32),
            pltpu.VMEM((lon - 1, piece, SUB, LANES), bf16),
            pltpu.VMEM((lon - 1, piece, SUB, LANES), bf16),
            pltpu.VMEM((piece, SUB, LANES), f32),
            pltpu.VMEM((pairs - 1, q, SUB, LANES), bf16),
            pltpu.VMEM((pairs - 1, q, SUB, LANES), bf16),
            dma((lon,)), dma((lon,)),
            dma((lon - 1,)), dma((lon - 1,)),
            dma((pairs - 1,)), dma((pairs - 1,)),
            dma((pairs - 1,)), dma((pairs - 1,)),
            dma((pairs, lon - 1)), dma((pairs, lon - 1)),
            dma((lon,)), dma((lon,)),
        ],
        compiler_params=pltpu.CompilerParams(
            collective_id=0, has_side_effects=True, vmem_limit_bytes=50 * 2**20
        ),
    )(features, cotangent, coef, weight.reshape(K * channels, channels))
    total = total[:used].astype(f32).reshape(K, channels // LANES, channels, LANES)
    grad_weight = jnp.swapaxes(total, 1, 2).reshape(weight.shape)
    return (mixed, grad_input, grad_weight)


def solution(mesh):
    return jax.shard_map(
        per_device,
        mesh=mesh,
        in_specs=(
            P("lat", "lon", None),
            P("lat", None, None),
            P("lat"),
            P("lat"),
            P(),
            P("lat", "lon", None),
        ),
        out_specs=(P("lat", "lon", None), P("lat", "lon", None), P()),
        check_vma=False,
    )
```

```python
import functools
import math

import jax
import jax.numpy as jnp
from jax import lax
from jax.experimental import pallas as pl
from jax.experimental.pallas import tpu as pltpu
from jax.sharding import PartitionSpec as P

K = 9
RAD = 2
WIDTH = 2 * RAD + 1
TAPS = WIDTH * WIDTH
J = 32
EDGE = 8
PAD = 16
WIN = J + 2 * EDGE
SUB, LANES = 16, 128
MESH = pl.DeviceIdType.MESH


def remote(src, dst, send, recv, device):
    copy = pltpu.make_async_remote_copy(
        src_ref=src, dst_ref=dst, send_sem=send, recv_sem=recv,
        device_id=device, device_id_type=MESH,
    )
    copy.start()
    return copy


def reduce_steps(
    lon, pairs, q, in_ref, out_ref, got_a, send_b, got_b, part, send_c, got_c,
    a_send, a_recv, b_send, b_recv, c_send, c_recv, d_send, d_recv, e_send, e_recv, f_send, f_recv,
):
    lat = lax.axis_index("lat")
    n = lax.axis_index("lon")
    core, z = lax.rem(lat, 2), lat // 2
    partner = (lat + 1 - 2 * core, n)
    piece = pairs * q
    half = lon * piece

    def lon_peer(s):
        return lax.rem(n + s, lon)

    def pair_peer(s):
        return lax.rem(z + s, pairs)

    theirs, mine = (1 - core) * half, core * half
    a_copies = []
    for s in range(lon):
        p = lon_peer(s + 1)
        a_copies.append(
            remote(
                in_ref.at[pl.ds(theirs + p * piece, piece)],
                got_a.at[pl.ds(p * piece, piece)],
                a_send.at[s], a_recv.at[s], partner,
            )
        )
    yield
    b_copies = []
    for s in range(lon):
        p = lon_peer(s + 1)
        a_copies[s].wait_recv()
        total = in_ref[pl.ds(mine + p * piece, piece)] + got_a[pl.ds(p * piece, piece)]
        if s < lon - 1:
            send_b[s] = total.astype(jnp.bfloat16)
            b_copies.append(remote(send_b.at[s], got_b.at[s], b_send.at[s], b_recv.at[s], (lat, p)))
        else:
            part[...] = total
    yield
    for s in range(lon - 1):
        b_copies[s].wait_recv()
        part[...] += got_b[s].astype(jnp.float32)
    c_copies = []
    for s in range(pairs - 1):
        p = pair_peer(s + 1)
        send_c[s] = part[pl.ds(p * q, q)].astype(jnp.bfloat16)
        c_copies.append(
            remote(send_c.at[s], got_c.at[s], c_send.at[s], c_recv.at[s], (p * 2 + core, n))
        )
    yield
    total = part[pl.ds(z * q, q)]
    for s in range(pairs - 1):
        c_copies[s].wait_recv()
        total = total + got_c[s].astype(jnp.float32)
    own = mine + n * piece
    out_ref[pl.ds(own + z * q, q)] = total.astype(jnp.bfloat16)

    d_copies, e_copies, f_copies = [], [], []

    def to_lon(t):
        src = out_ref.at[pl.ds(own + lax.rem(z + pairs - t, pairs) * q, q)]
        for s in range(lon - 1):
            e_copies.append(
                remote(src, src, e_send.at[t, s], e_recv.at[t, s], (lat, lon_peer(s + 1)))
            )

    def to_partner(s, p):
        src = out_ref.at[pl.ds(mine + p * piece, piece)]
        f_copies.append(remote(src, src, f_send.at[s], f_recv.at[s], partner))

    src = out_ref.at[pl.ds(own + z * q, q)]
    for s in range(pairs - 1):
        d_copies.append(
            remote(src, src, d_send.at[s], d_recv.at[s], (pair_peer(s + 1) * 2 + core, n))
        )
    to_lon(0)
    yield
    for t in range(1, pairs):
        d_copies[t - 1].wait_recv()
        to_lon(t)
    to_partner(0, n)
    yield
    for s in range(lon - 1):
        for t in range(pairs):
            e_copies[t * (lon - 1) + s].wait_recv()
        to_partner(s + 1, lax.rem(n + lon - s - 1, lon))
    yield
    for copy in f_copies:
        copy.wait_recv()
    for copy in a_copies + b_copies + c_copies + d_copies + e_copies + f_copies:
        copy.wait_send()


def halo_starts(src_ref, dst_ref, send, recv):
    rows, cols = src_ref.shape[0], src_ref.shape[1]
    lat, n = lax.axis_index("lat"), lax.axis_index("lon")
    lats, lons = lax.axis_size("lat"), lax.axis_size("lon")
    sides = {
        1: (pl.ds(rows - RAD, RAD), pl.ds(0, RAD)),
        0: (pl.ds(0, rows), pl.ds(RAD, rows)),
        -1: (pl.ds(0, RAD), pl.ds(RAD + rows, RAD)),
    }
    spans = {
        1: (pl.ds(cols - PAD, PAD), pl.ds(0, PAD)),
        0: (pl.ds(0, cols), pl.ds(PAD, cols)),
        -1: (pl.ds(0, PAD), pl.ds(PAD + cols, PAD)),
    }
    present = {1: lat < lats - 1, -1: lat > 0}
    copies = {1: [], 0: [], -1: []}
    for dy in (1, -1, 0):
        for dx in (0, 1, -1):
            if dy == 0 and dx == 0:
                continue
            slot = (dy + 1) * 3 + dx + 1
            copies[dy].append(
                pltpu.make_async_remote_copy(
                    src_ref=src_ref.at[sides[dy][0], spans[dx][0]],
                    dst_ref=dst_ref.at[sides[dy][1], spans[dx][1]],
                    send_sem=send.at[slot], recv_sem=recv.at[slot],
                    device_id=(lat + dy, lax.rem(n + dx + lons, lons)), device_id_type=MESH,
                )
            )
    for dy in (1, -1):
        @pl.when(present[dy])
        def _():
            for copy in copies[dy]:
                copy.start()
    for copy in copies[0]:
        copy.start()

    core = lax.rem(lat, 2)

    def wait(side, condition):
        @pl.when(condition)
        def _():
            for copy in copies[side]:
                copy.wait_recv()

    def near():
        for copy in copies[0]:
            copy.wait_recv()
        wait(-1, core == 0)
        wait(1, core == 1)

    def far():
        wait(1, (core == 0) & present[-1])
        wait(-1, (core == 1) & present[1])

    def sent():
        for copy in copies[0]:
            copy.wait_send()
        for dy in (1, -1):
            @pl.when(present[dy])
            def _():
                for copy in copies[dy]:
                    copy.wait_send()

    return near, far, sent


def kernel(
    scale, lon, pairs, q, f_ref, c_ref, basis_ref, lo_ref, hi_ref, w_hbm, mixed_hbm, gi_hbm, gw_ref,
    fx, cx, bx, w_ref, wt_ref, v_ref, u_ref, fa_ref, ca_ref, y_ref, ct_ref, mixed_ref, gi_ref,
    groups_ref, sums_ref, local_sem, f_send, f_recv, c_send, c_recv, b_send, b_recv, *reduce_scratch,
):
    rows, lon_count, channels = f_ref.shape
    lat, n = lax.axis_index("lat"), lax.axis_index("lon")
    lats = lax.axis_size("lat")
    core, z = lax.rem(lat, 2), lat // 2
    has = {1: lat < lats - 1, -1: lat > 0}

    barrier = pltpu.get_barrier_semaphore()
    for dy in (1, -1):
        @pl.when(has[dy])
        def _():
            for dx in (-1, 0, 1):
                there = (lat + dy, lax.rem(n + dx + lon, lon))
                pl.semaphore_signal(barrier, inc=1, device_id=there, device_id_type=MESH)
    for s in range(1, lon):
        there = (lat, lax.rem(n + s, lon))
        pl.semaphore_signal(barrier, inc=1, device_id=there, device_id_type=MESH)
    for s in range(1, pairs):
        there = (lax.rem(z + s, pairs) * 2 + core, n)
        pl.semaphore_signal(barrier, inc=1, device_id=there, device_id_type=MESH)
    here = pl.ds(RAD, rows)
    middle = pl.ds(PAD, lon_count)
    locals_ = [
        pltpu.make_async_copy(f_ref, fx.at[here, middle], local_sem.at[0]),
        pltpu.make_async_copy(c_ref, cx.at[here, middle], local_sem.at[1]),
        pltpu.make_async_copy(w_hbm, w_ref, local_sem.at[2]),
    ]
    for copy in locals_:
        copy.start()
    offset = lax.broadcasted_iota(jnp.int32, (K, TAPS), 1)
    offset = sum((offset >= m * WIDTH).astype(jnp.int32) for m in range(1, WIDTH)) - RAD
    bx[here] = jnp.zeros((rows,) + bx.shape[1:], jnp.float32)
    for i in range(rows):
        keep = (offset >= lo_ref[i]) & (offset <= hi_ref[i])
        bx[RAD + i, 0:K, 0:TAPS] = jnp.where(keep, basis_ref[i], 0.0)
    for dy, edge in ((1, 0), (-1, RAD + rows)):
        @pl.when(jnp.logical_not(has[-dy]))
        def _():
            fx[edge : edge + RAD] = jnp.zeros((RAD,) + fx.shape[1:], jnp.bfloat16)
            cx[edge : edge + RAD] = jnp.zeros((RAD,) + cx.shape[1:], jnp.bfloat16)
            bx[edge : edge + RAD] = jnp.zeros((RAD,) + bx.shape[1:], jnp.float32)
    pl.semaphore_wait(
        barrier,
        3 * has[1].astype(jnp.int32) + 3 * has[-1].astype(jnp.int32) + lon - 1 + pairs - 1,
    )

    f_near, f_far, f_sent = halo_starts(f_ref, fx, f_send, f_recv)
    b_copies = {}
    for slot, dy, src, dst in ((0, 1, rows, 0), (1, -1, RAD, RAD + rows)):
        b_copies[dy] = pltpu.make_async_remote_copy(
            src_ref=bx.at[pl.ds(src, RAD)], dst_ref=bx.at[pl.ds(dst, RAD)],
            send_sem=b_send.at[slot], recv_sem=b_recv.at[slot],
            device_id=(lat + dy, n), device_id_type=MESH,
        )

        @pl.when(has[dy])
        def _():
            b_copies[dy].start()

    taps = lax.broadcasted_iota(jnp.int32, (LANES, 256), 0)

    def segment(shape):
        lanes = lax.broadcasted_iota(jnp.int32, shape, 1)
        return sum((lanes >= m * WIN).astype(jnp.int32) for m in range(1, WIDTH))

    def pick(coef, want):
        chosen = jnp.where(taps == want, 1.0, 0.0).astype(jnp.bfloat16)
        out = jnp.dot(coef, chosen, preferred_element_type=jnp.float32)
        return out.reshape(coef.shape[0] // SUB, SUB, 256)

    def place(lines, a_ref, i):
        lane = lax.broadcasted_iota(jnp.int32, (J, 256), 1)
        row = lax.broadcasted_iota(jnp.int32, (J, 256), 0)
        col = lane - segment((J, 256)) * WIN - row - (EDGE - RAD)
        for k in range(K):
            a = jnp.zeros((J, 256), jnp.float32)
            for e in range(WIDTH):
                a = jnp.where(col == e, jnp.broadcast_to(lines[e][k : k + 1], (J, 256)), a)
            a_ref[i, k * J : (k + 1) * J] = a.astype(jnp.bfloat16)

    def build_forward():
        coef = bx[here].astype(jnp.bfloat16).reshape(rows * SUB, LANES)
        seg = segment((LANES, 256))
        for e in range(WIDTH):
            v_ref[e] = pick(coef, seg * WIDTH + e)

        def build(i, carry):
            place([v_ref[e, i] for e in range(WIDTH)], fa_ref, i)
            return carry

        lax.fori_loop(0, rows, build, 0)

    def build_adjoint():
        for dy in (1, -1):
            @pl.when(has[-dy])
            def _():
                b_copies[dy].wait_recv()
        coef = bx[...].astype(jnp.bfloat16).reshape((rows + 2 * RAD) * SUB, LANES)
        seg = segment((LANES, 256))
        for e in range(WIDTH):
            u_ref[e] = pick(coef, (WIDTH - 1 - seg) * WIDTH + WIDTH - 1 - e)
        seg = segment((SUB, 256))

        def build(i, carry):
            lines = []
            for e in range(WIDTH):
                line = u_ref[e, i]
                for r in range(1, WIDTH):
                    line = jnp.where(seg == r, u_ref[e, i + r], line)
                lines.append(line)
            place(lines, ca_ref, i)
            return carry

        lax.fori_loop(0, rows, build, 0)

    def stencil(x_ref, a_ref, i):
        a = a_ref[i][:, : WIDTH * WIN]
        for b in range(lon_count // J):
            x = x_ref[pl.ds(i, WIDTH), b * J : b * J + J + 2 * PAD, :]
            x = x[:, PAD - EDGE : PAD - EDGE + WIN].reshape(WIDTH * WIN, channels)
            y = jnp.dot(a, x, preferred_element_type=jnp.float32).astype(jnp.bfloat16)
            for k in range(K):
                y_ref[i, b * J : (b + 1) * J, k * channels : (k + 1) * channels] = y[k * J : (k + 1) * J]

    def mix(i, weights, out_ref):
        out_ref[i] = jnp.dot(
            y_ref[i], weights[...], preferred_element_type=jnp.float32
        ).astype(jnp.bfloat16)

    def looped(lo, hi, step):
        def body(i, carry):
            step(i)
            return carry

        lax.fori_loop(lo, hi, body, 0)

    halfway = rows // 2
    first_near = halfway * (1 - core)
    first_far = halfway * core
    build_forward()
    locals_[0].wait()
    f_near()
    looped(first_near, first_near + halfway, lambda i: stencil(fx, fa_ref, i))
    locals_[1].wait()
    for i in range(rows):
        ct_ref[:, i * lon_count : (i + 1) * lon_count] = cx[RAD + i, PAD : PAD + lon_count].T
    locals_[2].wait()
    looped(first_near, first_near + halfway, lambda i: mix(i, w_ref, mixed_ref))
    f_far()
    c_near, c_far, c_sent = halo_starts(c_ref, cx, c_send, c_recv)
    looped(first_far, first_far + halfway, lambda i: stencil(fx, fa_ref, i))

    chunks = groups_ref.shape[0]
    each = K // chunks
    per = channels // SUB
    halves = channels // LANES
    used = each * halves * per

    def product(m):
        for j in range(each):
            k = m * each + j
            total = jnp.zeros((channels, channels), jnp.float32)
            for i in range(rows):
                total += jnp.dot(
                    ct_ref[:, i * lon_count : (i + 1) * lon_count],
                    y_ref[i, :, k * channels : (k + 1) * channels],
                    preferred_element_type=jnp.float32,
                )
            turned = total.T * scale
            for h in range(halves):
                at = (j * halves + h) * per
                block = turned[:, h * LANES : (h + 1) * LANES]
                groups_ref[m, at : at + per] = block.reshape(per, SUB, LANES)
        rest = groups_ref.shape[1] - used
        if rest:
            groups_ref[m, used:] = jnp.zeros((rest, SUB, LANES), jnp.float32)

    def unpack(m):
        for j in range(each):
            k = m * each + j
            for h in range(halves):
                at = (j * halves + h) * per
                gw_ref[k * channels : (k + 1) * channels, h * LANES : (h + 1) * LANES] = sums_ref[
                    m, at : at + per
                ].reshape(channels, LANES)

    def reduction(m):
        scratch = [ref.at[m] for ref in reduce_scratch]
        yield from reduce_steps(lon, pairs, q, groups_ref.at[m], sums_ref.at[m], *scratch)
        unpack(m)

    sums = [reduction(m) for m in range(chunks)]

    def go(*which):
        for m in which:
            next(sums[m], None)

    out_copies = [
        pltpu.make_async_copy(mixed_ref, mixed_hbm, local_sem.at[3]),
        pltpu.make_async_copy(gi_ref, gi_hbm, local_sem.at[4]),
    ]

    def adjoint(i):
        stencil(cx, ca_ref, i)
        mix(i, wt_ref, gi_ref)

    product(0)
    go(0)
    product(1)
    go(1, 0)
    product(2)
    go(2, 1)
    looped(first_far, first_far + 1, lambda i: mix(i, w_ref, mixed_ref))
    go(2, 0)
    looped(first_far + 1, first_far + halfway, lambda i: mix(i, w_ref, mixed_ref))
    out_copies[0].start()
    go(1, 0)
    for k in range(K):
        block = slice(k * channels, (k + 1) * channels)
        wt_ref[block] = w_ref[block].T
    build_adjoint()
    go(2, 1, 0)
    c_near()
    looped(first_near, first_near + 1, adjoint)
    go(2, 1, 0)
    looped(first_near + 1, first_near + halfway, adjoint)
    go(2, 1, 0)
    c_far()
    looped(first_far, first_far + 1, adjoint)
    go(2, 1)
    looped(first_far + 1, first_far + halfway, adjoint)
    out_copies[1].start()
    for one in sums:
        for _ in one:
            pass
    f_sent()
    c_sent()
    for dy in (1, -1):
        @pl.when(has[dy])
        def _():
            b_copies[dy].wait_send()
    for copy in out_copies:
        copy.wait()


def per_device(features, basis, span_lo, span_hi, weight, cotangent):
    rows, lon_count, channels = features.shape
    scale = 1.0 / math.sqrt(rows * lax.axis_size("lat") * lon_count * lax.axis_size("lon"))
    lon, pairs = lax.axis_size("lon"), lax.axis_size("lat") // 2
    chunks = 3
    q = -(-weight.size // (SUB * LANES * chunks * 2 * lon * pairs))
    piece = pairs * q
    groups = 2 * lon * piece
    bf16, f32 = jnp.bfloat16, jnp.float32
    vmem = pl.BlockSpec(memory_space=pltpu.VMEM)
    smem = pl.BlockSpec(memory_space=pltpu.SMEM)
    anywhere = pl.BlockSpec(memory_space=pl.ANY)
    wide = (rows + 2 * RAD, lon_count + 2 * PAD, channels)

    def dma(*shape):
        return pltpu.SemaphoreType.DMA(shape)

    mixed, grad_input, total = pl.pallas_call(
        functools.partial(kernel, scale, lon, pairs, q),
        out_shape=(
            jax.ShapeDtypeStruct(features.shape, bf16),
            jax.ShapeDtypeStruct(features.shape, bf16),
            jax.ShapeDtypeStruct((K * channels, channels), bf16),
        ),
        in_specs=[anywhere, anywhere, vmem, smem, smem, anywhere],
        out_specs=[anywhere, anywhere, vmem],
        scratch_shapes=[
            pltpu.VMEM(wide, bf16),
            pltpu.VMEM(wide, bf16),
            pltpu.VMEM((rows + 2 * RAD, SUB, LANES), f32),
            pltpu.VMEM((K * channels, channels), bf16),
            pltpu.VMEM((K * channels, channels), bf16),
            pltpu.VMEM((WIDTH, rows, SUB, 256), f32),
            pltpu.VMEM((WIDTH, rows + 2 * RAD, SUB, 256), f32),
            pltpu.VMEM((rows, K * J, 256), bf16),
            pltpu.VMEM((rows, K * J, 256), bf16),
            pltpu.VMEM((rows, lon_count, K * channels), bf16),
            pltpu.VMEM((channels, rows * lon_count), bf16),
            pltpu.VMEM(features.shape, bf16),
            pltpu.VMEM(features.shape, bf16),
            pltpu.VMEM((chunks, groups, SUB, LANES), f32),
            pltpu.VMEM((chunks, groups, SUB, LANES), bf16),
            dma(5), dma(9), dma(9), dma(9), dma(9), dma(2), dma(2),
            pltpu.VMEM((chunks, lon * piece, SUB, LANES), f32),
            pltpu.VMEM((chunks, lon - 1, piece, SUB, LANES), bf16),
            pltpu.VMEM((chunks, lon - 1, piece, SUB, LANES), bf16),
            pltpu.VMEM((chunks, piece, SUB, LANES), f32),
            pltpu.VMEM((chunks, pairs - 1, q, SUB, LANES), bf16),
            pltpu.VMEM((chunks, pairs - 1, q, SUB, LANES), bf16),
            dma(chunks, lon), dma(chunks, lon),
            dma(chunks, lon - 1), dma(chunks, lon - 1),
            dma(chunks, pairs - 1), dma(chunks, pairs - 1),
            dma(chunks, pairs - 1), dma(chunks, pairs - 1),
            dma(chunks, pairs, lon - 1), dma(chunks, pairs, lon - 1),
            dma(chunks, lon), dma(chunks, lon),
        ],
        compiler_params=pltpu.CompilerParams(
            collective_id=0, has_side_effects=True, vmem_limit_bytes=60 * 2**20
        ),
    )(features, cotangent, basis, span_lo, span_hi, weight.reshape(K * channels, channels))
    return (mixed, grad_input, total.reshape(weight.shape).astype(f32))


def solution(mesh):
    return jax.shard_map(
        per_device,
        mesh=mesh,
        in_specs=(
            P("lat", "lon", None),
            P("lat", None, None),
            P("lat"),
            P("lat"),
            P(),
            P("lat", "lon", None),
        ),
        out_specs=(P("lat", "lon", None), P("lat", "lon", None), P()),
        check_vma=False,
    )
```

```python
import functools
import math

import jax
import jax.numpy as jnp
from jax import lax
from jax.experimental import pallas as pl
from jax.experimental.pallas import tpu as pltpu
from jax.sharding import PartitionSpec as P

K = 9
RAD = 2
WIDTH = 2 * RAD + 1
TAPS = WIDTH * WIDTH
J = 32
EDGE = 8
PAD = 16
WIN = J + 2 * EDGE
SUB, LANES = 16, 128
MESH = pl.DeviceIdType.MESH


def remote(src, dst, send, recv, device):
    copy = pltpu.make_async_remote_copy(
        src_ref=src, dst_ref=dst, send_sem=send, recv_sem=recv,
        device_id=device, device_id_type=MESH,
    )
    copy.start()
    return copy


def reduce_steps(
    lon, pairs, q, in_ref, out_ref, got_a, send_b, got_b, part, send_c, got_c,
    a_send, a_recv, b_send, b_recv, c_send, c_recv, d_send, d_recv, e_send, e_recv, f_send, f_recv,
):
    lat = lax.axis_index("lat")
    n = lax.axis_index("lon")
    core, z = lax.rem(lat, 2), lat // 2
    partner = (lat + 1 - 2 * core, n)
    piece = pairs * q
    half = lon * piece

    def lon_peer(s):
        return lax.rem(n + s, lon)

    def pair_peer(s):
        return lax.rem(z + s, pairs)

    theirs, mine = (1 - core) * half, core * half
    a_copies = []
    for s in range(lon):
        p = lon_peer(s + 1)
        a_copies.append(
            remote(
                in_ref.at[pl.ds(theirs + p * piece, piece)],
                got_a.at[pl.ds(p * piece, piece)],
                a_send.at[s], a_recv.at[s], partner,
            )
        )
    yield
    b_copies = []
    for s in range(lon):
        p = lon_peer(s + 1)
        a_copies[s].wait_recv()
        total = in_ref[pl.ds(mine + p * piece, piece)] + got_a[pl.ds(p * piece, piece)]
        if s < lon - 1:
            send_b[s] = total.astype(jnp.bfloat16)
            b_copies.append(remote(send_b.at[s], got_b.at[s], b_send.at[s], b_recv.at[s], (lat, p)))
        else:
            part[...] = total
    yield
    for s in range(lon - 1):
        b_copies[s].wait_recv()
        part[...] += got_b[s].astype(jnp.float32)
    c_copies = []
    for s in range(pairs - 1):
        p = pair_peer(s + 1)
        send_c[s] = part[pl.ds(p * q, q)].astype(jnp.bfloat16)
        c_copies.append(
            remote(send_c.at[s], got_c.at[s], c_send.at[s], c_recv.at[s], (p * 2 + core, n))
        )
    yield
    total = part[pl.ds(z * q, q)]
    for s in range(pairs - 1):
        c_copies[s].wait_recv()
        total = total + got_c[s].astype(jnp.float32)
    own = mine + n * piece
    out_ref[pl.ds(own + z * q, q)] = total.astype(jnp.bfloat16)

    d_copies, e_copies, f_copies = [], [], []

    def to_lon(t):
        src = out_ref.at[pl.ds(own + lax.rem(z + pairs - t, pairs) * q, q)]
        for s in range(lon - 1):
            e_copies.append(
                remote(src, src, e_send.at[t, s], e_recv.at[t, s], (lat, lon_peer(s + 1)))
            )

    def to_partner(s, p):
        src = out_ref.at[pl.ds(mine + p * piece, piece)]
        f_copies.append(remote(src, src, f_send.at[s], f_recv.at[s], partner))

    src = out_ref.at[pl.ds(own + z * q, q)]
    for s in range(pairs - 1):
        d_copies.append(
            remote(src, src, d_send.at[s], d_recv.at[s], (pair_peer(s + 1) * 2 + core, n))
        )
    to_lon(0)
    yield
    for t in range(1, pairs):
        d_copies[t - 1].wait_recv()
        to_lon(t)
    to_partner(0, n)
    yield
    for s in range(lon - 1):
        for t in range(pairs):
            e_copies[t * (lon - 1) + s].wait_recv()
        to_partner(s + 1, lax.rem(n + lon - s - 1, lon))
    yield
    for copy in f_copies:
        copy.wait_recv()
    for copy in a_copies + b_copies + c_copies + d_copies + e_copies + f_copies:
        copy.wait_send()


def halo_starts(src_ref, dst_ref, send, recv):
    rows, cols = src_ref.shape[0], src_ref.shape[1]
    lat, n = lax.axis_index("lat"), lax.axis_index("lon")
    lats, lons = lax.axis_size("lat"), lax.axis_size("lon")
    sides = {
        1: (pl.ds(rows - RAD, RAD), pl.ds(0, RAD)),
        0: (pl.ds(0, rows), pl.ds(RAD, rows)),
        -1: (pl.ds(0, RAD), pl.ds(RAD + rows, RAD)),
    }
    spans = {
        1: (pl.ds(cols - PAD, PAD), pl.ds(0, PAD)),
        0: (pl.ds(0, cols), pl.ds(PAD, cols)),
        -1: (pl.ds(0, PAD), pl.ds(PAD + cols, PAD)),
    }
    present = {1: lat < lats - 1, -1: lat > 0}
    copies = {1: [], 0: [], -1: []}
    for dy in (1, -1, 0):
        for dx in (0, 1, -1):
            if dy == 0 and dx == 0:
                continue
            slot = (dy + 1) * 3 + dx + 1
            copies[dy].append(
                pltpu.make_async_remote_copy(
                    src_ref=src_ref.at[sides[dy][0], spans[dx][0]],
                    dst_ref=dst_ref.at[sides[dy][1], spans[dx][1]],
                    send_sem=send.at[slot], recv_sem=recv.at[slot],
                    device_id=(lat + dy, lax.rem(n + dx + lons, lons)), device_id_type=MESH,
                )
            )
    for dy in (1, -1):
        @pl.when(present[dy])
        def _():
            for copy in copies[dy]:
                copy.start()
    for copy in copies[0]:
        copy.start()

    core = lax.rem(lat, 2)

    def wait(side, condition):
        @pl.when(condition)
        def _():
            for copy in copies[side]:
                copy.wait_recv()

    def near():
        for copy in copies[0]:
            copy.wait_recv()
        wait(-1, core == 0)
        wait(1, core == 1)

    def far():
        wait(1, (core == 0) & present[-1])
        wait(-1, (core == 1) & present[1])

    def sent():
        for copy in copies[0]:
            copy.wait_send()
        for dy in (1, -1):
            @pl.when(present[dy])
            def _():
                for copy in copies[dy]:
                    copy.wait_send()

    return near, far, sent


def kernel(
    scale, lon, pairs, q, f_ref, c_ref, basis_ref, lo_ref, hi_ref, w_hbm, mixed_hbm, gi_hbm, gw_ref,
    fx, cx, bx, w_ref, wt_ref, v_ref, u_ref, fa_ref, ca_ref, y_ref, ct_ref, mixed_ref, gi_ref,
    acc_ref, groups_ref, sums_ref, local_sem, f_send, f_recv, c_send, c_recv, b_send, b_recv, *reduce_scratch,
):
    rows, lon_count, channels = f_ref.shape
    lat, n = lax.axis_index("lat"), lax.axis_index("lon")
    lats = lax.axis_size("lat")
    core, z = lax.rem(lat, 2), lat // 2
    has = {1: lat < lats - 1, -1: lat > 0}

    barrier = pltpu.get_barrier_semaphore()
    for dy in (1, -1):
        @pl.when(has[dy])
        def _():
            for dx in (-1, 0, 1):
                there = (lat + dy, lax.rem(n + dx + lon, lon))
                pl.semaphore_signal(barrier, inc=1, device_id=there, device_id_type=MESH)
    for s in range(1, lon):
        there = (lat, lax.rem(n + s, lon))
        pl.semaphore_signal(barrier, inc=1, device_id=there, device_id_type=MESH)
    for s in range(1, pairs):
        there = (lax.rem(z + s, pairs) * 2 + core, n)
        pl.semaphore_signal(barrier, inc=1, device_id=there, device_id_type=MESH)
    here = pl.ds(RAD, rows)
    middle = pl.ds(PAD, lon_count)
    locals_ = [
        pltpu.make_async_copy(f_ref, fx.at[here, middle], local_sem.at[0]),
        pltpu.make_async_copy(c_ref, cx.at[here, middle], local_sem.at[1]),
        pltpu.make_async_copy(w_hbm, w_ref, local_sem.at[2]),
    ]
    for copy in locals_:
        copy.start()
    offset = lax.broadcasted_iota(jnp.int32, (K, TAPS), 1)
    offset = sum((offset >= m * WIDTH).astype(jnp.int32) for m in range(1, WIDTH)) - RAD
    bx[here] = jnp.zeros((rows,) + bx.shape[1:], jnp.float32)
    for i in range(rows):
        keep = (offset >= lo_ref[i]) & (offset <= hi_ref[i])
        bx[RAD + i, 0:K, 0:TAPS] = jnp.where(keep, basis_ref[:, i, :], 0.0)
    for dy, edge in ((1, 0), (-1, RAD + rows)):
        @pl.when(jnp.logical_not(has[-dy]))
        def _():
            fx[edge : edge + RAD] = jnp.zeros((RAD,) + fx.shape[1:], jnp.bfloat16)
            cx[edge : edge + RAD] = jnp.zeros((RAD,) + cx.shape[1:], jnp.bfloat16)
            bx[edge : edge + RAD] = jnp.zeros((RAD,) + bx.shape[1:], jnp.float32)
    pl.semaphore_wait(
        barrier,
        3 * has[1].astype(jnp.int32) + 3 * has[-1].astype(jnp.int32) + lon - 1 + pairs - 1,
    )

    b_copies = {}
    for slot, dy, src, dst in ((0, 1, rows, 0), (1, -1, RAD, RAD + rows)):
        b_copies[dy] = pltpu.make_async_remote_copy(
            src_ref=bx.at[pl.ds(src, RAD)], dst_ref=bx.at[pl.ds(dst, RAD)],
            send_sem=b_send.at[slot], recv_sem=b_recv.at[slot],
            device_id=(lat + dy, n), device_id_type=MESH,
        )

        @pl.when(has[dy])
        def _():
            b_copies[dy].start()

    f_near, f_far, f_sent = halo_starts(f_ref, fx, f_send, f_recv)

    taps = lax.broadcasted_iota(jnp.int32, (LANES, 256), 0)

    def segment(shape):
        lanes = lax.broadcasted_iota(jnp.int32, shape, 1)
        return sum((lanes >= m * WIN).astype(jnp.int32) for m in range(1, WIDTH))

    def pick(coef, want):
        chosen = jnp.where(taps == want, 1.0, 0.0).astype(jnp.bfloat16)
        out = jnp.dot(coef, chosen, preferred_element_type=jnp.float32)
        return out.reshape(coef.shape[0] // SUB, SUB, 256)

    def place(lines, a_ref, i):
        lane = lax.broadcasted_iota(jnp.int32, (J, 256), 1)
        row = lax.broadcasted_iota(jnp.int32, (J, 256), 0)
        col = lane - segment((J, 256)) * WIN - row - (EDGE - RAD)
        for k in range(K):
            a = jnp.zeros((J, 256), jnp.float32)
            for e in range(WIDTH):
                a = jnp.where(col == e, jnp.broadcast_to(lines[e][k : k + 1], (J, 256)), a)
            a_ref[i, k * J : (k + 1) * J] = a.astype(jnp.bfloat16)

    def build_forward():
        coef = bx[here].astype(jnp.bfloat16).reshape(rows * SUB, LANES)
        seg = segment((LANES, 256))
        for e in range(WIDTH):
            v_ref[e] = pick(coef, seg * WIDTH + e)

        def build(i, carry):
            place([v_ref[e, i] for e in range(WIDTH)], fa_ref, i)
            return carry

        lax.fori_loop(0, rows, build, 0)

    def build_adjoint():
        for dy in (1, -1):
            @pl.when(has[-dy])
            def _():
                b_copies[dy].wait_recv()
        coef = bx[...].astype(jnp.bfloat16).reshape((rows + 2 * RAD) * SUB, LANES)
        seg = segment((LANES, 256))
        for e in range(WIDTH):
            u_ref[e] = pick(coef, (WIDTH - 1 - seg) * WIDTH + WIDTH - 1 - e)
        seg = segment((SUB, 256))

        def build(i, carry):
            lines = []
            for e in range(WIDTH):
                line = u_ref[e, i]
                for r in range(1, WIDTH):
                    line = jnp.where(seg == r, u_ref[e, i + r], line)
                lines.append(line)
            place(lines, ca_ref, i)
            return carry

        lax.fori_loop(0, rows, build, 0)

    def stencil(x_ref, a_ref, i):
        a = a_ref[i][:, : WIDTH * WIN]
        for b in range(lon_count // J):
            x = x_ref[pl.ds(i, WIDTH), b * J : b * J + J + 2 * PAD, :]
            x = x[:, PAD - EDGE : PAD - EDGE + WIN].reshape(WIDTH * WIN, channels)
            y = jnp.dot(a, x, preferred_element_type=jnp.float32).astype(jnp.bfloat16)
            for k in range(K):
                y_ref[i, b * J : (b + 1) * J, k * channels : (k + 1) * channels] = y[k * J : (k + 1) * J]

    def mix(i, weights, out_ref):
        out_ref[i] = jnp.dot(
            y_ref[i], weights[...], preferred_element_type=jnp.float32
        ).astype(jnp.bfloat16)

    def looped(lo, hi, step):
        def body(i, carry):
            step(i)
            return carry

        lax.fori_loop(lo, hi, body, 0)

    halfway = rows // 2
    first_near = halfway * (1 - core)
    first_far = halfway * core
    build_forward()
    locals_[0].wait()
    f_near()
    looped(first_near, first_near + halfway, lambda i: stencil(fx, fa_ref, i))
    locals_[1].wait()
    for i in range(rows):
        ct_ref[i] = cx[RAD + i, PAD : PAD + lon_count].T

    def product(k, first):
        column = slice(k * channels, (k + 1) * channels)
        total = jnp.zeros((channels, channels), jnp.float32)
        for r in range(halfway):
            total += jnp.dot(
                ct_ref[first + r], y_ref[first + r, :, column], preferred_element_type=jnp.float32
            )
        return total

    for k in range(K):
        acc_ref[k] = product(k, first_near)
    locals_[2].wait()
    for k in range(K):
        block = slice(k * channels, (k + 1) * channels)
        wt_ref[block] = w_ref[block].T
    f_far()
    c_near, c_far, c_sent = halo_starts(c_ref, cx, c_send, c_recv)
    looped(first_far, first_far + halfway, lambda i: stencil(fx, fa_ref, i))

    chunks = groups_ref.shape[0]
    each = K // chunks
    per = channels // SUB
    halves = channels // LANES
    used = each * halves * per

    def chunk(m):
        for j in range(each):
            k = m * each + j
            turned = (acc_ref[k] + product(k, first_far)).T * scale
            for h in range(halves):
                at = (j * halves + h) * per
                block = turned[:, h * LANES : (h + 1) * LANES]
                groups_ref[m, at : at + per] = block.reshape(per, SUB, LANES)
        rest = groups_ref.shape[1] - used
        if rest:
            groups_ref[m, used:] = jnp.zeros((rest, SUB, LANES), jnp.float32)

    def unpack(m):
        for j in range(each):
            k = m * each + j
            for h in range(halves):
                at = (j * halves + h) * per
                gw_ref[k * channels : (k + 1) * channels, h * LANES : (h + 1) * LANES] = sums_ref[
                    m, at : at + per
                ].reshape(channels, LANES)

    def reduction(m):
        scratch = [ref.at[m] for ref in reduce_scratch]
        yield from reduce_steps(lon, pairs, q, groups_ref.at[m], sums_ref.at[m], *scratch)
        unpack(m)

    sums = [reduction(m) for m in range(chunks)]

    def go(*which):
        for m in which:
            next(sums[m], None)

    out_copies = [
        pltpu.make_async_copy(mixed_ref, mixed_hbm, local_sem.at[3]),
        pltpu.make_async_copy(gi_ref, gi_hbm, local_sem.at[4]),
    ]

    def adjoint(i):
        stencil(cx, ca_ref, i)
        mix(i, wt_ref, gi_ref)

    chunk(0)
    go(0)
    chunk(1)
    go(1, 0)
    chunk(2)
    go(2, 1)
    looped(first_near, first_near + halfway, lambda i: mix(i, w_ref, mixed_ref))
    go(2, 0)
    looped(first_far, first_far + halfway, lambda i: mix(i, w_ref, mixed_ref))
    out_copies[0].start()
    go(1, 0)
    build_adjoint()
    go(2, 1, 0)
    c_near()
    looped(first_near, first_near + 1, adjoint)
    go(2, 1, 0)
    looped(first_near + 1, first_near + halfway, adjoint)
    go(2, 1, 0)
    c_far()
    looped(first_far, first_far + 1, adjoint)
    go(2, 1)
    looped(first_far + 1, first_far + halfway, adjoint)
    out_copies[1].start()
    for one in sums:
        for _ in one:
            pass
    f_sent()
    c_sent()
    for dy in (1, -1):
        @pl.when(has[dy])
        def _():
            b_copies[dy].wait_send()
    for copy in out_copies:
        copy.wait()


def finish_kernel(
    mixed_in, gi_in, sums_in, mixed_out, gi_out, gw_out, narrow, wide, moved, loaded, stored
):
    loads = [pltpu.make_async_copy(sums_in.at[k], narrow.at[k], loaded.at[k]) for k in range(K)]
    for copy in loads:
        copy.start()
    moves = [
        pltpu.make_async_copy(mixed_in, mixed_out, moved.at[0]),
        pltpu.make_async_copy(gi_in, gi_out, moved.at[1]),
    ]
    for copy in moves:
        copy.start()
    stores = []
    for k in range(K):
        loads[k].wait()
        wide[k] = narrow[k].astype(jnp.float32)
        stores.append(pltpu.make_async_copy(wide.at[k], gw_out.at[k], stored.at[k]))
        stores[k].start()
    for copy in moves + stores:
        copy.wait()


def per_device(features, basis, span_lo, span_hi, weight, cotangent):
    rows, lon_count, channels = features.shape
    scale = 1.0 / math.sqrt(rows * lax.axis_size("lat") * lon_count * lax.axis_size("lon"))
    lon, pairs = lax.axis_size("lon"), lax.axis_size("lat") // 2
    chunks = 3
    q = -(-weight.size // (SUB * LANES * chunks * 2 * lon * pairs))
    piece = pairs * q
    groups = 2 * lon * piece
    bf16, f32 = jnp.bfloat16, jnp.float32
    vmem = pl.BlockSpec(memory_space=pltpu.VMEM)
    smem = pl.BlockSpec(memory_space=pltpu.SMEM)
    anywhere = pl.BlockSpec(memory_space=pl.ANY)
    wide = (rows + 2 * RAD, lon_count + 2 * PAD, channels)

    def dma(*shape):
        return pltpu.SemaphoreType.DMA(shape)

    mixed, grad_input, total = pl.pallas_call(
        functools.partial(kernel, scale, lon, pairs, q),
        out_shape=(
            jax.ShapeDtypeStruct(features.shape, bf16),
            jax.ShapeDtypeStruct(features.shape, bf16),
            jax.ShapeDtypeStruct((K * channels, channels), bf16),
        ),
        in_specs=[anywhere, anywhere, vmem, smem, smem, anywhere],
        out_specs=[anywhere, anywhere, vmem],
        scratch_shapes=[
            pltpu.VMEM(wide, bf16),
            pltpu.VMEM(wide, bf16),
            pltpu.VMEM((rows + 2 * RAD, SUB, LANES), f32),
            pltpu.VMEM((K * channels, channels), bf16),
            pltpu.VMEM((K * channels, channels), bf16),
            pltpu.VMEM((WIDTH, rows, SUB, 256), f32),
            pltpu.VMEM((WIDTH, rows + 2 * RAD, SUB, 256), f32),
            pltpu.VMEM((rows, K * J, 256), bf16),
            pltpu.VMEM((rows, K * J, 256), bf16),
            pltpu.VMEM((rows, lon_count, K * channels), bf16),
            pltpu.VMEM((rows, channels, lon_count), bf16),
            pltpu.VMEM(features.shape, bf16),
            pltpu.VMEM(features.shape, bf16),
            pltpu.VMEM((K, channels, channels), f32),
            pltpu.VMEM((chunks, groups, SUB, LANES), f32),
            pltpu.VMEM((chunks, groups, SUB, LANES), bf16),
            dma(5), dma(9), dma(9), dma(9), dma(9), dma(2), dma(2),
            pltpu.VMEM((chunks, lon * piece, SUB, LANES), f32),
            pltpu.VMEM((chunks, lon - 1, piece, SUB, LANES), bf16),
            pltpu.VMEM((chunks, lon - 1, piece, SUB, LANES), bf16),
            pltpu.VMEM((chunks, piece, SUB, LANES), f32),
            pltpu.VMEM((chunks, pairs - 1, q, SUB, LANES), bf16),
            pltpu.VMEM((chunks, pairs - 1, q, SUB, LANES), bf16),
            dma(chunks, lon), dma(chunks, lon),
            dma(chunks, lon - 1), dma(chunks, lon - 1),
            dma(chunks, pairs - 1), dma(chunks, pairs - 1),
            dma(chunks, pairs - 1), dma(chunks, pairs - 1),
            dma(chunks, pairs, lon - 1), dma(chunks, pairs, lon - 1),
            dma(chunks, lon), dma(chunks, lon),
        ],
        compiler_params=pltpu.CompilerParams(
            collective_id=0, has_side_effects=True, vmem_limit_bytes=60 * 2**20
        ),
    )(features, cotangent, jnp.swapaxes(basis, 0, 1), span_lo, span_hi, weight.reshape(K * channels, channels))
    return pl.pallas_call(
        finish_kernel,
        out_shape=(
            jax.ShapeDtypeStruct(features.shape, bf16),
            jax.ShapeDtypeStruct(features.shape, bf16),
            jax.ShapeDtypeStruct(weight.shape, f32),
        ),
        in_specs=[anywhere] * 3,
        out_specs=[anywhere] * 3,
        scratch_shapes=[
            pltpu.VMEM(weight.shape, bf16),
            pltpu.VMEM(weight.shape, f32),
            dma(2), dma(K), dma(K),
        ],
        compiler_params=pltpu.CompilerParams(vmem_limit_bytes=60 * 2**20),
    )(mixed, grad_input, total.reshape(weight.shape))


def solution(mesh):
    return jax.shard_map(
        per_device,
        mesh=mesh,
        in_specs=(
            P("lat", "lon", None),
            P("lat", None, None),
            P("lat"),
            P("lat"),
            P(),
            P("lat", "lon", None),
        ),
        out_specs=(P("lat", "lon", None), P("lat", "lon", None), P()),
        check_vma=False,
    )
```

```python
import functools
import math

import jax
import jax.numpy as jnp
from jax import lax
from jax.experimental import pallas as pl
from jax.experimental.pallas import tpu as pltpu
from jax.sharding import PartitionSpec as P

K = 9
RAD = 2
WIDTH = 2 * RAD + 1
TAPS = WIDTH * WIDTH
J = 32
EDGE = 8
PAD = 16
WIN = J + 2 * EDGE
SUB, LANES = 16, 128
MESH = pl.DeviceIdType.MESH


def remote(src, dst, send, recv, device):
    copy = pltpu.make_async_remote_copy(
        src_ref=src, dst_ref=dst, send_sem=send, recv_sem=recv,
        device_id=device, device_id_type=MESH,
    )
    copy.start()
    return copy


def reduce_steps(
    lon, pairs, q, in_ref, out_ref, got_a, send_b, got_b, part, send_c, got_c,
    a_send, a_recv, b_send, b_recv, c_send, c_recv, d_send, d_recv, e_send, e_recv, f_send, f_recv,
):
    lat = lax.axis_index("lat")
    n = lax.axis_index("lon")
    core, z = lax.rem(lat, 2), lat // 2
    partner = (lat + 1 - 2 * core, n)
    piece = pairs * q
    half = lon * piece

    def lon_peer(s):
        return lax.rem(n + s, lon)

    def pair_peer(s):
        return lax.rem(z + s, pairs)

    theirs, mine = (1 - core) * half, core * half
    a_copies = []
    for s in range(lon):
        p = lon_peer(s + 1)
        a_copies.append(
            remote(
                in_ref.at[pl.ds(theirs + p * piece, piece)],
                got_a.at[pl.ds(p * piece, piece)],
                a_send.at[s], a_recv.at[s], partner,
            )
        )
    yield
    b_copies = []
    for s in range(lon):
        p = lon_peer(s + 1)
        a_copies[s].wait_recv()
        total = in_ref[pl.ds(mine + p * piece, piece)] + got_a[pl.ds(p * piece, piece)]
        if s < lon - 1:
            send_b[s] = total.astype(jnp.bfloat16)
            b_copies.append(remote(send_b.at[s], got_b.at[s], b_send.at[s], b_recv.at[s], (lat, p)))
        else:
            part[...] = total
    yield
    for s in range(lon - 1):
        b_copies[s].wait_recv()
        part[...] += got_b[s].astype(jnp.float32)
    c_copies = []
    for s in range(pairs - 1):
        p = pair_peer(s + 1)
        send_c[s] = part[pl.ds(p * q, q)].astype(jnp.bfloat16)
        c_copies.append(
            remote(send_c.at[s], got_c.at[s], c_send.at[s], c_recv.at[s], (p * 2 + core, n))
        )
    yield
    total = part[pl.ds(z * q, q)]
    for s in range(pairs - 1):
        c_copies[s].wait_recv()
        total = total + got_c[s].astype(jnp.float32)
    own = mine + n * piece
    out_ref[pl.ds(own + z * q, q)] = total.astype(jnp.bfloat16)

    d_copies, e_copies, f_copies = [], [], []

    def to_lon(t):
        src = out_ref.at[pl.ds(own + lax.rem(z + pairs - t, pairs) * q, q)]
        for s in range(lon - 1):
            e_copies.append(
                remote(src, src, e_send.at[t, s], e_recv.at[t, s], (lat, lon_peer(s + 1)))
            )

    def to_partner(s, p):
        src = out_ref.at[pl.ds(mine + p * piece, piece)]
        f_copies.append(remote(src, src, f_send.at[s], f_recv.at[s], partner))

    src = out_ref.at[pl.ds(own + z * q, q)]
    for s in range(pairs - 1):
        d_copies.append(
            remote(src, src, d_send.at[s], d_recv.at[s], (pair_peer(s + 1) * 2 + core, n))
        )
    to_lon(0)
    yield
    for t in range(1, pairs):
        d_copies[t - 1].wait_recv()
        to_lon(t)
    to_partner(0, n)
    yield
    for s in range(lon - 1):
        for t in range(pairs):
            e_copies[t * (lon - 1) + s].wait_recv()
        to_partner(s + 1, lax.rem(n + lon - s - 1, lon))
    yield
    for copy in f_copies:
        copy.wait_recv()
    for copy in a_copies + b_copies + c_copies + d_copies + e_copies + f_copies:
        copy.wait_send()


def halo_starts(src_ref, dst_ref, send, recv):
    rows, cols = src_ref.shape[0], src_ref.shape[1]
    lat, n = lax.axis_index("lat"), lax.axis_index("lon")
    lats, lons = lax.axis_size("lat"), lax.axis_size("lon")
    sides = {
        1: (pl.ds(rows - RAD, RAD), pl.ds(0, RAD)),
        0: (pl.ds(0, rows), pl.ds(RAD, rows)),
        -1: (pl.ds(0, RAD), pl.ds(RAD + rows, RAD)),
    }
    spans = {
        1: (pl.ds(cols - PAD, PAD), pl.ds(0, PAD)),
        0: (pl.ds(0, cols), pl.ds(PAD, cols)),
        -1: (pl.ds(0, PAD), pl.ds(PAD + cols, PAD)),
    }
    present = {1: lat < lats - 1, -1: lat > 0}
    copies = {1: [], 0: [], -1: []}
    for dy in (1, -1, 0):
        for dx in (0, 1, -1):
            if dy == 0 and dx == 0:
                continue
            slot = (dy + 1) * 3 + dx + 1
            copies[dy].append(
                pltpu.make_async_remote_copy(
                    src_ref=src_ref.at[sides[dy][0], spans[dx][0]],
                    dst_ref=dst_ref.at[sides[dy][1], spans[dx][1]],
                    send_sem=send.at[slot], recv_sem=recv.at[slot],
                    device_id=(lat + dy, lax.rem(n + dx + lons, lons)), device_id_type=MESH,
                )
            )
    for dy in (1, -1):
        @pl.when(present[dy])
        def _():
            for copy in copies[dy]:
                copy.start()
    for copy in copies[0]:
        copy.start()

    core = lax.rem(lat, 2)

    def wait(side, condition):
        @pl.when(condition)
        def _():
            for copy in copies[side]:
                copy.wait_recv()

    def near():
        for copy in copies[0]:
            copy.wait_recv()
        wait(-1, core == 0)
        wait(1, core == 1)

    def far():
        wait(1, (core == 0) & present[-1])
        wait(-1, (core == 1) & present[1])

    def sent():
        for copy in copies[0]:
            copy.wait_send()
        for dy in (1, -1):
            @pl.when(present[dy])
            def _():
                for copy in copies[dy]:
                    copy.wait_send()

    return near, far, sent


def kernel(
    scale, lon, pairs, q, f_ref, c_ref, basis_ref, lo_ref, hi_ref, w_hbm, mixed_hbm, gi_hbm, gw_ref,
    fx, cx, bx, w_ref, wt_ref, v_ref, u_ref, fa_ref, ca_ref, y_ref, ct_ref, mixed_ref, gi_ref,
    acc_ref, groups_ref, sums_ref, local_sem, f_send, f_recv, c_send, c_recv, b_send, b_recv, *reduce_scratch,
):
    rows, lon_count, channels = f_ref.shape
    lat, n = lax.axis_index("lat"), lax.axis_index("lon")
    lats = lax.axis_size("lat")
    core, z = lax.rem(lat, 2), lat // 2
    has = {1: lat < lats - 1, -1: lat > 0}

    barrier = pltpu.get_barrier_semaphore()
    for dy in (1, -1):
        @pl.when(has[dy])
        def _():
            for dx in (-1, 0, 1):
                there = (lat + dy, lax.rem(n + dx + lon, lon))
                pl.semaphore_signal(barrier, inc=1, device_id=there, device_id_type=MESH)
    for s in range(1, lon):
        there = (lat, lax.rem(n + s, lon))
        pl.semaphore_signal(barrier, inc=1, device_id=there, device_id_type=MESH)
    for s in range(1, pairs):
        there = (lax.rem(z + s, pairs) * 2 + core, n)
        pl.semaphore_signal(barrier, inc=1, device_id=there, device_id_type=MESH)
    here = pl.ds(RAD, rows)
    middle = pl.ds(PAD, lon_count)
    locals_ = [
        pltpu.make_async_copy(f_ref, fx.at[here, middle], local_sem.at[0]),
        pltpu.make_async_copy(c_ref, cx.at[here, middle], local_sem.at[1]),
        pltpu.make_async_copy(w_hbm, w_ref, local_sem.at[2]),
    ]
    for copy in locals_:
        copy.start()
    offset = lax.broadcasted_iota(jnp.int32, (K, TAPS), 1)
    offset = sum((offset >= m * WIDTH).astype(jnp.int32) for m in range(1, WIDTH)) - RAD
    bx[here] = jnp.zeros((rows,) + bx.shape[1:], jnp.float32)
    for i in range(rows):
        keep = (offset >= lo_ref[i]) & (offset <= hi_ref[i])
        bx[RAD + i, 0:K, 0:TAPS] = jnp.where(keep, basis_ref[:, i, :], 0.0)
    for dy, edge in ((1, 0), (-1, RAD + rows)):
        @pl.when(jnp.logical_not(has[-dy]))
        def _():
            fx[edge : edge + RAD] = jnp.zeros((RAD,) + fx.shape[1:], jnp.bfloat16)
            cx[edge : edge + RAD] = jnp.zeros((RAD,) + cx.shape[1:], jnp.bfloat16)
            bx[edge : edge + RAD] = jnp.zeros((RAD,) + bx.shape[1:], jnp.float32)
    pl.semaphore_wait(
        barrier,
        3 * has[1].astype(jnp.int32) + 3 * has[-1].astype(jnp.int32) + lon - 1 + pairs - 1,
    )

    b_copies = {}
    for slot, dy, src, dst in ((0, 1, rows, 0), (1, -1, RAD, RAD + rows)):
        b_copies[dy] = pltpu.make_async_remote_copy(
            src_ref=bx.at[pl.ds(src, RAD)], dst_ref=bx.at[pl.ds(dst, RAD)],
            send_sem=b_send.at[slot], recv_sem=b_recv.at[slot],
            device_id=(lat + dy, n), device_id_type=MESH,
        )

        @pl.when(has[dy])
        def _():
            b_copies[dy].start()

    f_near, f_far, f_sent = halo_starts(f_ref, fx, f_send, f_recv)

    taps = lax.broadcasted_iota(jnp.int32, (LANES, 256), 0)

    def segment(shape):
        lanes = lax.broadcasted_iota(jnp.int32, shape, 1)
        return sum((lanes >= m * WIN).astype(jnp.int32) for m in range(1, WIDTH))

    def pick(coef, want):
        chosen = jnp.where(taps == want, 1.0, 0.0).astype(jnp.bfloat16)
        out = jnp.dot(coef, chosen, preferred_element_type=jnp.float32)
        return out.reshape(coef.shape[0] // SUB, SUB, 256)

    def place(lines, a_ref, i):
        lane = lax.broadcasted_iota(jnp.int32, (J, 256), 1)
        row = lax.broadcasted_iota(jnp.int32, (J, 256), 0)
        col = lane - segment((J, 256)) * WIN - row - (EDGE - RAD)
        for k in range(K):
            a = jnp.zeros((J, 256), jnp.float32)
            for e in range(WIDTH):
                a = jnp.where(col == e, jnp.broadcast_to(lines[e][k : k + 1], (J, 256)), a)
            a_ref[i, k * J : (k + 1) * J] = a.astype(jnp.bfloat16)

    def build_forward():
        coef = bx[here].astype(jnp.bfloat16).reshape(rows * SUB, LANES)
        seg = segment((LANES, 256))
        for e in range(WIDTH):
            v_ref[e] = pick(coef, seg * WIDTH + e)

        def build(i, carry):
            place([v_ref[e, i] for e in range(WIDTH)], fa_ref, i)
            return carry

        lax.fori_loop(0, rows, build, 0)

    def build_adjoint():
        for dy in (1, -1):
            @pl.when(has[-dy])
            def _():
                b_copies[dy].wait_recv()
        coef = bx[...].astype(jnp.bfloat16).reshape((rows + 2 * RAD) * SUB, LANES)
        seg = segment((LANES, 256))
        for e in range(WIDTH):
            u_ref[e] = pick(coef, (WIDTH - 1 - seg) * WIDTH + WIDTH - 1 - e)
        seg = segment((SUB, 256))

        def build(i, carry):
            lines = []
            for e in range(WIDTH):
                line = u_ref[e, i]
                for r in range(1, WIDTH):
                    line = jnp.where(seg == r, u_ref[e, i + r], line)
                lines.append(line)
            place(lines, ca_ref, i)
            return carry

        lax.fori_loop(0, rows, build, 0)

    def stencil(x_ref, a_ref, i):
        a = a_ref[i][:, : WIDTH * WIN]
        for b in range(lon_count // J):
            x = x_ref[pl.ds(i, WIDTH), b * J : b * J + J + 2 * PAD, :]
            x = x[:, PAD - EDGE : PAD - EDGE + WIN].reshape(WIDTH * WIN, channels)
            y = jnp.dot(a, x, preferred_element_type=jnp.float32).astype(jnp.bfloat16)
            for k in range(K):
                y_ref[i, b * J : (b + 1) * J, k * channels : (k + 1) * channels] = y[k * J : (k + 1) * J]

    def mix(i, weights, out_ref):
        out_ref[i] = jnp.dot(
            y_ref[i], weights[...], preferred_element_type=jnp.float32
        ).astype(jnp.bfloat16)

    def looped(lo, hi, step):
        def body(i, carry):
            step(i)
            return carry

        lax.fori_loop(lo, hi, body, 0)

    halfway = rows // 2
    first_near = halfway * (1 - core)
    first_far = halfway * core
    build_forward()
    locals_[0].wait()
    f_near()
    looped(first_near, first_near + halfway, lambda i: stencil(fx, fa_ref, i))
    locals_[1].wait()
    for i in range(rows):
        ct_ref[i] = cx[RAD + i, PAD : PAD + lon_count].T

    def product(k, first):
        column = slice(k * channels, (k + 1) * channels)
        total = jnp.zeros((channels, channels), jnp.float32)
        for r in range(halfway):
            total += jnp.dot(
                ct_ref[first + r], y_ref[first + r, :, column], preferred_element_type=jnp.float32
            )
        return total

    for k in range(K):
        acc_ref[k] = product(k, first_near)
    locals_[2].wait()
    for k in range(K):
        block = slice(k * channels, (k + 1) * channels)
        wt_ref[block] = w_ref[block].T
    f_far()
    c_near, c_far, c_sent = halo_starts(c_ref, cx, c_send, c_recv)
    looped(first_far, first_far + halfway, lambda i: stencil(fx, fa_ref, i))

    chunks = groups_ref.shape[0]
    each = K // chunks
    per = channels // SUB
    halves = channels // LANES
    used = each * halves * per

    def chunk(m):
        for j in range(each):
            k = m * each + j
            turned = (acc_ref[k] + product(k, first_far)).T * scale
            for h in range(halves):
                at = (j * halves + h) * per
                block = turned[:, h * LANES : (h + 1) * LANES]
                groups_ref[m, at : at + per] = block.reshape(per, SUB, LANES)
        rest = groups_ref.shape[1] - used
        if rest:
            groups_ref[m, used:] = jnp.zeros((rest, SUB, LANES), jnp.float32)

    def unpack(m):
        for j in range(each):
            k = m * each + j
            for h in range(halves):
                at = (j * halves + h) * per
                gw_ref[k * channels : (k + 1) * channels, h * LANES : (h + 1) * LANES] = sums_ref[
                    m, at : at + per
                ].reshape(channels, LANES)

    def reduction(m):
        scratch = [ref.at[m] for ref in reduce_scratch]
        yield from reduce_steps(lon, pairs, q, groups_ref.at[m], sums_ref.at[m], *scratch)
        unpack(m)

    sums = [reduction(m) for m in range(chunks)]

    def go(*which):
        for m in which:
            next(sums[m], None)

    out_copies = [
        pltpu.make_async_copy(mixed_ref, mixed_hbm, local_sem.at[3]),
        pltpu.make_async_copy(gi_ref, gi_hbm, local_sem.at[4]),
    ]

    def adjoint(i):
        stencil(cx, ca_ref, i)
        mix(i, wt_ref, gi_ref)

    chunk(0)
    go(0)
    chunk(1)
    go(1, 0)
    chunk(2)
    go(2, 1)
    looped(first_near, first_near + halfway, lambda i: mix(i, w_ref, mixed_ref))
    go(2, 0)
    looped(first_far, first_far + halfway, lambda i: mix(i, w_ref, mixed_ref))
    out_copies[0].start()
    go(1, 0)
    build_adjoint()
    go(2, 1, 0)
    c_near()
    looped(first_near, first_near + 1, adjoint)
    go(2, 1, 0)
    looped(first_near + 1, first_near + halfway, adjoint)
    go(2, 1, 0)
    c_far()
    looped(first_far, first_far + 1, adjoint)
    go(2, 1)
    looped(first_far + 1, first_far + halfway, adjoint)
    out_copies[1].start()
    for one in sums:
        for _ in one:
            pass
    f_sent()
    c_sent()
    for dy in (1, -1):
        @pl.when(has[dy])
        def _():
            b_copies[dy].wait_send()
    for copy in out_copies:
        copy.wait()


def finish_kernel(
    mixed_in, gi_in, sums_in, mixed_out, gi_out, gw_out, mixed, gi, narrow, wide,
    moved_in, moved_out, loaded, stored,
):
    rows = mixed.shape[0]
    loads, stores = [], []
    for a, (src, held, dst) in enumerate(((mixed_in, mixed, mixed_out), (gi_in, gi, gi_out))):
        for i in range(rows):
            loads.append(pltpu.make_async_copy(src.at[i], held.at[i], moved_in.at[a, i]))
            stores.append(pltpu.make_async_copy(held.at[i], dst.at[i], moved_out.at[a, i]))
    sums = [pltpu.make_async_copy(sums_in.at[k], narrow.at[k], loaded.at[k]) for k in range(K)]
    for copy in sums + loads:
        copy.start()
    for k in range(K):
        sums[k].wait()
        wide[k] = narrow[k].astype(jnp.float32)
        copy = pltpu.make_async_copy(wide.at[k], gw_out.at[k], stored.at[k])
        copy.start()
        stores.append(copy)
    for i, copy in enumerate(loads):
        copy.wait()
        stores[i].start()
    for copy in stores:
        copy.wait()


def per_device(features, basis, span_lo, span_hi, weight, cotangent):
    rows, lon_count, channels = features.shape
    scale = 1.0 / math.sqrt(rows * lax.axis_size("lat") * lon_count * lax.axis_size("lon"))
    lon, pairs = lax.axis_size("lon"), lax.axis_size("lat") // 2
    chunks = 3
    q = -(-weight.size // (SUB * LANES * chunks * 2 * lon * pairs))
    piece = pairs * q
    groups = 2 * lon * piece
    bf16, f32 = jnp.bfloat16, jnp.float32
    vmem = pl.BlockSpec(memory_space=pltpu.VMEM)
    smem = pl.BlockSpec(memory_space=pltpu.SMEM)
    anywhere = pl.BlockSpec(memory_space=pl.ANY)
    wide = (rows + 2 * RAD, lon_count + 2 * PAD, channels)

    def dma(*shape):
        return pltpu.SemaphoreType.DMA(shape)

    mixed, grad_input, total = pl.pallas_call(
        functools.partial(kernel, scale, lon, pairs, q),
        out_shape=(
            jax.ShapeDtypeStruct(features.shape, bf16),
            jax.ShapeDtypeStruct(features.shape, bf16),
            jax.ShapeDtypeStruct((K * channels, channels), bf16),
        ),
        in_specs=[anywhere, anywhere, vmem, smem, smem, anywhere],
        out_specs=[anywhere, anywhere, vmem],
        scratch_shapes=[
            pltpu.VMEM(wide, bf16),
            pltpu.VMEM(wide, bf16),
            pltpu.VMEM((rows + 2 * RAD, SUB, LANES), f32),
            pltpu.VMEM((K * channels, channels), bf16),
            pltpu.VMEM((K * channels, channels), bf16),
            pltpu.VMEM((WIDTH, rows, SUB, 256), f32),
            pltpu.VMEM((WIDTH, rows + 2 * RAD, SUB, 256), f32),
            pltpu.VMEM((rows, K * J, 256), bf16),
            pltpu.VMEM((rows, K * J, 256), bf16),
            pltpu.VMEM((rows, lon_count, K * channels), bf16),
            pltpu.VMEM((rows, channels, lon_count), bf16),
            pltpu.VMEM(features.shape, bf16),
            pltpu.VMEM(features.shape, bf16),
            pltpu.VMEM((K, channels, channels), f32),
            pltpu.VMEM((chunks, groups, SUB, LANES), f32),
            pltpu.VMEM((chunks, groups, SUB, LANES), bf16),
            dma(5), dma(9), dma(9), dma(9), dma(9), dma(2), dma(2),
            pltpu.VMEM((chunks, lon * piece, SUB, LANES), f32),
            pltpu.VMEM((chunks, lon - 1, piece, SUB, LANES), bf16),
            pltpu.VMEM((chunks, lon - 1, piece, SUB, LANES), bf16),
            pltpu.VMEM((chunks, piece, SUB, LANES), f32),
            pltpu.VMEM((chunks, pairs - 1, q, SUB, LANES), bf16),
            pltpu.VMEM((chunks, pairs - 1, q, SUB, LANES), bf16),
            dma(chunks, lon), dma(chunks, lon),
            dma(chunks, lon - 1), dma(chunks, lon - 1),
            dma(chunks, pairs - 1), dma(chunks, pairs - 1),
            dma(chunks, pairs - 1), dma(chunks, pairs - 1),
            dma(chunks, pairs, lon - 1), dma(chunks, pairs, lon - 1),
            dma(chunks, lon), dma(chunks, lon),
        ],
        compiler_params=pltpu.CompilerParams(
            collective_id=0, has_side_effects=True, vmem_limit_bytes=60 * 2**20
        ),
    )(features, cotangent, jnp.swapaxes(basis, 0, 1), span_lo, span_hi, weight.reshape(K * channels, channels))
    return pl.pallas_call(
        finish_kernel,
        out_shape=(
            jax.ShapeDtypeStruct(features.shape, bf16),
            jax.ShapeDtypeStruct(features.shape, bf16),
            jax.ShapeDtypeStruct(weight.shape, f32),
        ),
        in_specs=[anywhere] * 3,
        out_specs=[anywhere] * 3,
        scratch_shapes=[
            pltpu.VMEM(features.shape, bf16),
            pltpu.VMEM(features.shape, bf16),
            pltpu.VMEM(weight.shape, bf16),
            pltpu.VMEM(weight.shape, f32),
            dma(2, rows), dma(2, rows), dma(K), dma(K),
        ],
        compiler_params=pltpu.CompilerParams(vmem_limit_bytes=60 * 2**20),
    )(mixed, grad_input, total.reshape(weight.shape))


def solution(mesh):
    return jax.shard_map(
        per_device,
        mesh=mesh,
        in_specs=(
            P("lat", "lon", None),
            P("lat", None, None),
            P("lat"),
            P("lat"),
            P(),
            P("lat", "lon", None),
        ),
        out_specs=(P("lat", "lon", None), P("lat", "lon", None), P()),
        check_vma=False,
    )
```

```python
import functools
import math

import jax
import jax.numpy as jnp
from jax import lax
from jax.experimental import pallas as pl
from jax.experimental.pallas import tpu as pltpu
from jax.sharding import PartitionSpec as P

K = 9
RAD = 2
WIDTH = 2 * RAD + 1
TAPS = WIDTH * WIDTH
J = 32
EDGE = 8
PAD = 16
WIN = J + 2 * EDGE
SUB, LANES = 16, 128
MESH = pl.DeviceIdType.MESH


def remote(src, dst, send, recv, device):
    copy = pltpu.make_async_remote_copy(
        src_ref=src, dst_ref=dst, send_sem=send, recv_sem=recv,
        device_id=device, device_id_type=MESH,
    )
    copy.start()
    return copy


def reduce_steps(
    lon, pairs, q, in_ref, out_ref, got_a, send_b, got_b, part, send_c, got_c,
    a_send, a_recv, b_send, b_recv, c_send, c_recv, d_send, d_recv, e_send, e_recv, f_send, f_recv,
):
    lat = lax.axis_index("lat")
    n = lax.axis_index("lon")
    core, z = lax.rem(lat, 2), lat // 2
    partner = (lat + 1 - 2 * core, n)
    piece = pairs * q
    half = lon * piece

    def lon_peer(s):
        return lax.rem(n + s, lon)

    def pair_peer(s):
        return lax.rem(z + s, pairs)

    theirs, mine = (1 - core) * half, core * half
    a_copies = []
    for s in range(lon):
        p = lon_peer(s + 1)
        a_copies.append(
            remote(
                in_ref.at[pl.ds(theirs + p * piece, piece)],
                got_a.at[pl.ds(p * piece, piece)],
                a_send.at[s], a_recv.at[s], partner,
            )
        )
    yield
    b_copies = []
    for s in range(lon):
        p = lon_peer(s + 1)
        a_copies[s].wait_recv()
        total = in_ref[pl.ds(mine + p * piece, piece)] + got_a[pl.ds(p * piece, piece)]
        if s < lon - 1:
            send_b[s] = total.astype(jnp.bfloat16)
            b_copies.append(remote(send_b.at[s], got_b.at[s], b_send.at[s], b_recv.at[s], (lat, p)))
        else:
            part[...] = total
    yield
    for s in range(lon - 1):
        b_copies[s].wait_recv()
        part[...] += got_b[s].astype(jnp.float32)
    c_copies = []
    for s in range(pairs - 1):
        p = pair_peer(s + 1)
        send_c[s] = part[pl.ds(p * q, q)].astype(jnp.bfloat16)
        c_copies.append(
            remote(send_c.at[s], got_c.at[s], c_send.at[s], c_recv.at[s], (p * 2 + core, n))
        )
    yield
    total = part[pl.ds(z * q, q)]
    for s in range(pairs - 1):
        c_copies[s].wait_recv()
        total = total + got_c[s].astype(jnp.float32)
    own = mine + n * piece
    out_ref[pl.ds(own + z * q, q)] = total.astype(jnp.bfloat16)

    d_copies, e_copies, f_copies = [], [], []

    def to_partner(s, p):
        src = out_ref.at[pl.ds(mine + p * piece, piece)]
        f_copies.append(remote(src, src, f_send.at[s], f_recv.at[s], partner))

    src = out_ref.at[pl.ds(own + z * q, q)]
    for s in range(pairs - 1):
        d_copies.append(
            remote(src, src, d_send.at[s], d_recv.at[s], (pair_peer(s + 1) * 2 + core, n))
        )
    yield
    for copy in d_copies:
        copy.wait_recv()
    src = out_ref.at[pl.ds(own, piece)]
    for s in range(lon - 1):
        e_copies.append(remote(src, src, e_send.at[s], e_recv.at[s], (lat, lon_peer(s + 1))))
    to_partner(0, n)
    yield
    for s in range(lon - 1):
        e_copies[s].wait_recv()
        to_partner(s + 1, lax.rem(n + lon - s - 1, lon))
    yield
    for copy in f_copies:
        copy.wait_recv()
    for copy in a_copies + b_copies + c_copies + d_copies + e_copies + f_copies:
        copy.wait_send()


def halo_starts(src_ref, dst_ref, send, recv):
    rows, cols = src_ref.shape[0], src_ref.shape[1]
    lat, n = lax.axis_index("lat"), lax.axis_index("lon")
    lats, lons = lax.axis_size("lat"), lax.axis_size("lon")
    sides = {
        1: (pl.ds(rows - RAD, RAD), pl.ds(0, RAD)),
        0: (pl.ds(0, rows), pl.ds(RAD, rows)),
        -1: (pl.ds(0, RAD), pl.ds(RAD + rows, RAD)),
    }
    spans = {
        1: (pl.ds(cols - PAD, PAD), pl.ds(0, PAD)),
        0: (pl.ds(0, cols), pl.ds(PAD, cols)),
        -1: (pl.ds(0, PAD), pl.ds(PAD + cols, PAD)),
    }
    present = {1: lat < lats - 1, -1: lat > 0}
    copies = {1: [], 0: [], -1: []}
    for dy in (1, -1, 0):
        for dx in (0, 1, -1):
            if dy == 0 and dx == 0:
                continue
            slot = (dy + 1) * 3 + dx + 1
            copies[dy].append(
                pltpu.make_async_remote_copy(
                    src_ref=src_ref.at[sides[dy][0], spans[dx][0]],
                    dst_ref=dst_ref.at[sides[dy][1], spans[dx][1]],
                    send_sem=send.at[slot], recv_sem=recv.at[slot],
                    device_id=(lat + dy, lax.rem(n + dx + lons, lons)), device_id_type=MESH,
                )
            )
    for dy in (1, -1):
        @pl.when(present[dy])
        def _():
            for copy in copies[dy]:
                copy.start()
    for copy in copies[0]:
        copy.start()

    core = lax.rem(lat, 2)

    def wait(side, condition):
        @pl.when(condition)
        def _():
            for copy in copies[side]:
                copy.wait_recv()

    def near():
        for copy in copies[0]:
            copy.wait_recv()
        wait(-1, core == 0)
        wait(1, core == 1)

    def far():
        wait(1, (core == 0) & present[-1])
        wait(-1, (core == 1) & present[1])

    def sent():
        for copy in copies[0]:
            copy.wait_send()
        for dy in (1, -1):
            @pl.when(present[dy])
            def _():
                for copy in copies[dy]:
                    copy.wait_send()

    return near, far, sent


def kernel(
    scale, lon, pairs, q, f_ref, c_ref, basis_ref, lo_ref, hi_ref, w_hbm, mixed_hbm, gi_hbm, gw_ref,
    fx, cx, bx, w_ref, wt_ref, v_ref, u_ref, fa_ref, ca_ref, y_ref, ct_ref, mixed_ref, gi_ref,
    acc_ref, groups_ref, sums_ref, local_sem, f_send, f_recv, c_send, c_recv, b_send, b_recv, *reduce_scratch,
):
    rows, lon_count, channels = f_ref.shape
    lat, n = lax.axis_index("lat"), lax.axis_index("lon")
    lats = lax.axis_size("lat")
    core, z = lax.rem(lat, 2), lat // 2
    has = {1: lat < lats - 1, -1: lat > 0}

    barrier = pltpu.get_barrier_semaphore()
    for dy in (1, -1):
        @pl.when(has[dy])
        def _():
            for dx in (-1, 0, 1):
                there = (lat + dy, lax.rem(n + dx + lon, lon))
                pl.semaphore_signal(barrier, inc=1, device_id=there, device_id_type=MESH)
    for s in range(1, lon):
        there = (lat, lax.rem(n + s, lon))
        pl.semaphore_signal(barrier, inc=1, device_id=there, device_id_type=MESH)
    for s in range(1, pairs):
        there = (lax.rem(z + s, pairs) * 2 + core, n)
        pl.semaphore_signal(barrier, inc=1, device_id=there, device_id_type=MESH)
    here = pl.ds(RAD, rows)
    middle = pl.ds(PAD, lon_count)
    locals_ = [
        pltpu.make_async_copy(f_ref, fx.at[here, middle], local_sem.at[0]),
        pltpu.make_async_copy(c_ref, cx.at[here, middle], local_sem.at[1]),
        pltpu.make_async_copy(w_hbm, w_ref, local_sem.at[2]),
    ]
    for copy in locals_:
        copy.start()
    offset = lax.broadcasted_iota(jnp.int32, (K, TAPS), 1)
    offset = sum((offset >= m * WIDTH).astype(jnp.int32) for m in range(1, WIDTH)) - RAD
    bx[here] = jnp.zeros((rows,) + bx.shape[1:], jnp.float32)
    for i in range(rows):
        keep = (offset >= lo_ref[i]) & (offset <= hi_ref[i])
        bx[RAD + i, 0:K, 0:TAPS] = jnp.where(keep, basis_ref[:, i, :], 0.0)
    for dy, edge in ((1, 0), (-1, RAD + rows)):
        @pl.when(jnp.logical_not(has[-dy]))
        def _():
            fx[edge : edge + RAD] = jnp.zeros((RAD,) + fx.shape[1:], jnp.bfloat16)
            cx[edge : edge + RAD] = jnp.zeros((RAD,) + cx.shape[1:], jnp.bfloat16)
            bx[edge : edge + RAD] = jnp.zeros((RAD,) + bx.shape[1:], jnp.float32)
    pl.semaphore_wait(
        barrier,
        3 * has[1].astype(jnp.int32) + 3 * has[-1].astype(jnp.int32) + lon - 1 + pairs - 1,
    )

    b_copies = {}
    for slot, dy, src, dst in ((0, 1, rows, 0), (1, -1, RAD, RAD + rows)):
        b_copies[dy] = pltpu.make_async_remote_copy(
            src_ref=bx.at[pl.ds(src, RAD)], dst_ref=bx.at[pl.ds(dst, RAD)],
            send_sem=b_send.at[slot], recv_sem=b_recv.at[slot],
            device_id=(lat + dy, n), device_id_type=MESH,
        )

        @pl.when(has[dy])
        def _():
            b_copies[dy].start()

    f_near, f_far, f_sent = halo_starts(f_ref, fx, f_send, f_recv)

    taps = lax.broadcasted_iota(jnp.int32, (LANES, 256), 0)

    def segment(shape):
        lanes = lax.broadcasted_iota(jnp.int32, shape, 1)
        return sum((lanes >= m * WIN).astype(jnp.int32) for m in range(1, WIDTH))

    def pick(coef, want):
        chosen = jnp.where(taps == want, 1.0, 0.0).astype(jnp.bfloat16)
        out = jnp.dot(coef, chosen, preferred_element_type=jnp.float32)
        return out.reshape(coef.shape[0] // SUB, SUB, 256)

    def place(lines, a_ref, i):
        lane = lax.broadcasted_iota(jnp.int32, (J, 256), 1)
        row = lax.broadcasted_iota(jnp.int32, (J, 256), 0)
        col = lane - segment((J, 256)) * WIN - row - (EDGE - RAD)
        for k in range(K):
            a = jnp.zeros((J, 256), jnp.float32)
            for e in range(WIDTH):
                a = jnp.where(col == e, jnp.broadcast_to(lines[e][k : k + 1], (J, 256)), a)
            a_ref[i, k * J : (k + 1) * J] = a.astype(jnp.bfloat16)

    def build_forward():
        coef = bx[here].astype(jnp.bfloat16).reshape(rows * SUB, LANES)
        seg = segment((LANES, 256))
        for e in range(WIDTH):
            v_ref[e] = pick(coef, seg * WIDTH + e)

        def build(i, carry):
            place([v_ref[e, i] for e in range(WIDTH)], fa_ref, i)
            return carry

        lax.fori_loop(0, rows, build, 0)

    def build_adjoint():
        for dy in (1, -1):
            @pl.when(has[-dy])
            def _():
                b_copies[dy].wait_recv()
        coef = bx[...].astype(jnp.bfloat16).reshape((rows + 2 * RAD) * SUB, LANES)
        seg = segment((LANES, 256))
        for e in range(WIDTH):
            u_ref[e] = pick(coef, (WIDTH - 1 - seg) * WIDTH + WIDTH - 1 - e)
        seg = segment((SUB, 256))

        def build(i, carry):
            lines = []
            for e in range(WIDTH):
                line = u_ref[e, i]
                for r in range(1, WIDTH):
                    line = jnp.where(seg == r, u_ref[e, i + r], line)
                lines.append(line)
            place(lines, ca_ref, i)
            return carry

        lax.fori_loop(0, rows, build, 0)

    def stencil(x_ref, a_ref, i):
        a = a_ref[i][:, : WIDTH * WIN]
        for b in range(lon_count // J):
            x = x_ref[pl.ds(i, WIDTH), b * J : b * J + J + 2 * PAD, :]
            x = x[:, PAD - EDGE : PAD - EDGE + WIN].reshape(WIDTH * WIN, channels)
            y = jnp.dot(a, x, preferred_element_type=jnp.float32).astype(jnp.bfloat16)
            for k in range(K):
                y_ref[i, b * J : (b + 1) * J, k * channels : (k + 1) * channels] = y[k * J : (k + 1) * J]

    def mix(i, weights, out_ref):
        out_ref[i] = jnp.dot(
            y_ref[i], weights[...], preferred_element_type=jnp.float32
        ).astype(jnp.bfloat16)

    def looped(lo, hi, step):
        def body(i, carry):
            step(i)
            return carry

        lax.fori_loop(lo, hi, body, 0)

    halfway = rows // 2
    first_near = halfway * (1 - core)
    first_far = halfway * core
    build_forward()
    locals_[0].wait()
    f_near()
    looped(first_near, first_near + halfway, lambda i: stencil(fx, fa_ref, i))
    locals_[1].wait()
    for i in range(rows):
        ct_ref[i] = cx[RAD + i, PAD : PAD + lon_count].T

    def product(k, first):
        column = slice(k * channels, (k + 1) * channels)
        total = jnp.zeros((channels, channels), jnp.float32)
        for r in range(halfway):
            total += jnp.dot(
                ct_ref[first + r], y_ref[first + r, :, column], preferred_element_type=jnp.float32
            )
        return total

    for k in range(K):
        acc_ref[k] = product(k, first_near)
    locals_[2].wait()
    for k in range(K):
        block = slice(k * channels, (k + 1) * channels)
        wt_ref[block] = w_ref[block].T
    f_far()
    c_near, c_far, c_sent = halo_starts(c_ref, cx, c_send, c_recv)
    looped(first_far, first_far + halfway, lambda i: stencil(fx, fa_ref, i))

    chunks = groups_ref.shape[0]
    each = K // chunks
    per = channels // SUB
    halves = channels // LANES
    used = each * halves * per

    def chunk(m):
        for j in range(each):
            k = m * each + j
            turned = (acc_ref[k] + product(k, first_far)).T * scale
            for h in range(halves):
                at = (j * halves + h) * per
                block = turned[:, h * LANES : (h + 1) * LANES]
                groups_ref[m, at : at + per] = block.reshape(per, SUB, LANES)
        rest = groups_ref.shape[1] - used
        if rest:
            groups_ref[m, used:] = jnp.zeros((rest, SUB, LANES), jnp.float32)

    def unpack(m):
        for j in range(each):
            k = m * each + j
            for h in range(halves):
                at = (j * halves + h) * per
                gw_ref[k * channels : (k + 1) * channels, h * LANES : (h + 1) * LANES] = sums_ref[
                    m, at : at + per
                ].reshape(channels, LANES)

    def reduction(m):
        scratch = [ref.at[m] for ref in reduce_scratch]
        yield from reduce_steps(lon, pairs, q, groups_ref.at[m], sums_ref.at[m], *scratch)
        unpack(m)

    sums = [reduction(m) for m in range(chunks)]

    def go(*which):
        for m in which:
            next(sums[m], None)

    out_copies = [
        pltpu.make_async_copy(mixed_ref, mixed_hbm, local_sem.at[3]),
        pltpu.make_async_copy(gi_ref, gi_hbm, local_sem.at[4]),
    ]

    def adjoint(i):
        stencil(cx, ca_ref, i)
        mix(i, wt_ref, gi_ref)

    chunk(0)
    go(0)
    chunk(1)
    go(1, 0)
    chunk(2)
    go(2, 1)
    looped(first_near, first_near + halfway, lambda i: mix(i, w_ref, mixed_ref))
    go(2, 0)
    looped(first_far, first_far + halfway, lambda i: mix(i, w_ref, mixed_ref))
    out_copies[0].start()
    go(1, 0)
    build_adjoint()
    go(2, 1, 0)
    c_near()
    looped(first_near, first_near + 1, adjoint)
    go(2, 1, 0)
    looped(first_near + 1, first_near + halfway, adjoint)
    go(2, 1, 0)
    c_far()
    looped(first_far, first_far + 1, adjoint)
    go(2, 1)
    looped(first_far + 1, first_far + halfway, adjoint)
    out_copies[1].start()
    for one in sums:
        for _ in one:
            pass
    f_sent()
    c_sent()
    for dy in (1, -1):
        @pl.when(has[dy])
        def _():
            b_copies[dy].wait_send()
    for copy in out_copies:
        copy.wait()


def finish_kernel(
    mixed_in, gi_in, sums_in, mixed_out, gi_out, gw_out, mixed, gi, narrow, wide,
    moved_in, moved_out, loaded, stored,
):
    rows = mixed.shape[0]
    loads, stores = [], []
    for a, (src, held, dst) in enumerate(((mixed_in, mixed, mixed_out), (gi_in, gi, gi_out))):
        for i in range(rows):
            loads.append(pltpu.make_async_copy(src.at[i], held.at[i], moved_in.at[a, i]))
            stores.append(pltpu.make_async_copy(held.at[i], dst.at[i], moved_out.at[a, i]))
    sums = [pltpu.make_async_copy(sums_in.at[k], narrow.at[k], loaded.at[k]) for k in range(K)]
    for copy in sums + loads:
        copy.start()
    for k in range(K):
        sums[k].wait()
        wide[k] = narrow[k].astype(jnp.float32)
        copy = pltpu.make_async_copy(wide.at[k], gw_out.at[k], stored.at[k])
        copy.start()
        stores.append(copy)
    for i, copy in enumerate(loads):
        copy.wait()
        stores[i].start()
    for copy in stores:
        copy.wait()


def per_device(features, basis, span_lo, span_hi, weight, cotangent):
    rows, lon_count, channels = features.shape
    scale = 1.0 / math.sqrt(rows * lax.axis_size("lat") * lon_count * lax.axis_size("lon"))
    lon, pairs = lax.axis_size("lon"), lax.axis_size("lat") // 2
    chunks = 3
    q = -(-weight.size // (SUB * LANES * chunks * 2 * lon * pairs))
    piece = pairs * q
    groups = 2 * lon * piece
    bf16, f32 = jnp.bfloat16, jnp.float32
    vmem = pl.BlockSpec(memory_space=pltpu.VMEM)
    smem = pl.BlockSpec(memory_space=pltpu.SMEM)
    anywhere = pl.BlockSpec(memory_space=pl.ANY)
    wide = (rows + 2 * RAD, lon_count + 2 * PAD, channels)

    def dma(*shape):
        return pltpu.SemaphoreType.DMA(shape)

    mixed, grad_input, total = pl.pallas_call(
        functools.partial(kernel, scale, lon, pairs, q),
        out_shape=(
            jax.ShapeDtypeStruct(features.shape, bf16),
            jax.ShapeDtypeStruct(features.shape, bf16),
            jax.ShapeDtypeStruct((K * channels, channels), bf16),
        ),
        in_specs=[anywhere, anywhere, vmem, smem, smem, anywhere],
        out_specs=[anywhere, anywhere, vmem],
        scratch_shapes=[
            pltpu.VMEM(wide, bf16),
            pltpu.VMEM(wide, bf16),
            pltpu.VMEM((rows + 2 * RAD, SUB, LANES), f32),
            pltpu.VMEM((K * channels, channels), bf16),
            pltpu.VMEM((K * channels, channels), bf16),
            pltpu.VMEM((WIDTH, rows, SUB, 256), f32),
            pltpu.VMEM((WIDTH, rows + 2 * RAD, SUB, 256), f32),
            pltpu.VMEM((rows, K * J, 256), bf16),
            pltpu.VMEM((rows, K * J, 256), bf16),
            pltpu.VMEM((rows, lon_count, K * channels), bf16),
            pltpu.VMEM((rows, channels, lon_count), bf16),
            pltpu.VMEM(features.shape, bf16),
            pltpu.VMEM(features.shape, bf16),
            pltpu.VMEM((K, channels, channels), f32),
            pltpu.VMEM((chunks, groups, SUB, LANES), f32),
            pltpu.VMEM((chunks, groups, SUB, LANES), bf16),
            dma(5), dma(9), dma(9), dma(9), dma(9), dma(2), dma(2),
            pltpu.VMEM((chunks, lon * piece, SUB, LANES), f32),
            pltpu.VMEM((chunks, lon - 1, piece, SUB, LANES), bf16),
            pltpu.VMEM((chunks, lon - 1, piece, SUB, LANES), bf16),
            pltpu.VMEM((chunks, piece, SUB, LANES), f32),
            pltpu.VMEM((chunks, pairs - 1, q, SUB, LANES), bf16),
            pltpu.VMEM((chunks, pairs - 1, q, SUB, LANES), bf16),
            dma(chunks, lon), dma(chunks, lon),
            dma(chunks, lon - 1), dma(chunks, lon - 1),
            dma(chunks, pairs - 1), dma(chunks, pairs - 1),
            dma(chunks, pairs - 1), dma(chunks, pairs - 1),
            dma(chunks, lon - 1), dma(chunks, lon - 1),
            dma(chunks, lon), dma(chunks, lon),
        ],
        compiler_params=pltpu.CompilerParams(
            collective_id=0, has_side_effects=True, vmem_limit_bytes=60 * 2**20
        ),
    )(features, cotangent, jnp.swapaxes(basis, 0, 1), span_lo, span_hi, weight.reshape(K * channels, channels))
    return pl.pallas_call(
        finish_kernel,
        out_shape=(
            jax.ShapeDtypeStruct(features.shape, bf16),
            jax.ShapeDtypeStruct(features.shape, bf16),
            jax.ShapeDtypeStruct(weight.shape, f32),
        ),
        in_specs=[anywhere] * 3,
        out_specs=[anywhere] * 3,
        scratch_shapes=[
            pltpu.VMEM(features.shape, bf16),
            pltpu.VMEM(features.shape, bf16),
            pltpu.VMEM(weight.shape, bf16),
            pltpu.VMEM(weight.shape, f32),
            dma(2, rows), dma(2, rows), dma(K), dma(K),
        ],
        compiler_params=pltpu.CompilerParams(vmem_limit_bytes=60 * 2**20),
    )(mixed, grad_input, total.reshape(weight.shape))


def solution(mesh):
    return jax.shard_map(
        per_device,
        mesh=mesh,
        in_specs=(
            P("lat", "lon", None),
            P("lat", None, None),
            P("lat"),
            P("lat"),
            P(),
            P("lat", "lon", None),
        ),
        out_specs=(P("lat", "lon", None), P("lat", "lon", None), P()),
        check_vma=False,
    )
```
